512 devices in a mesh: pipe: 16 (over z, x_lo), expert: 32 (over y, x_hi, core).
Axes of the slice: x: 4 (x_hi: 2, x_lo: 2; x = x_hi * 2 + x_lo), y: 8, z: 8, core: 2. Of those that a mesh axis runs over, the one named last changes fastest.
Arguments:
- fwd_tokens: bfloat16 [16, 2048, 3584], P('pipe', 'expert'), may hold values from -6 to 6
- bwd_tokens: bfloat16 [16, 2048, 3584], P('pipe', 'expert'), may hold values from -6 to 6
- bwd_cotangent: bfloat16 [16, 2048, 3584], P('pipe', 'expert'), may hold values from -6 to 6
- fwd_routes: int32 [16, 2048, 8], P('pipe', 'expert'), may hold values from 0 to 255, as said below
- bwd_routes: int32 [16, 2048, 8], P('pipe', 'expert'), may hold values from 0 to 255, as said below
- router_weight: bfloat16 [16, 3584, 256], P('pipe', 'expert'), may hold values from -0.09375 to 0.09375
- up_weight: bfloat16 [16, 3584, 4096], P('pipe', None, 'expert'), may hold values from -0.09375 to 0.09375
- down_weight: bfloat16 [16, 4096, 3584], P('pipe', 'expert'), may hold values from -0.1875 to 0.1875
Outputs:
- fwd_next: bfloat16 [16, 2048, 3584], P('pipe', 'expert')
- bwd_next: bfloat16 [16, 2048, 3584], P('pipe', 'expert')
The draws below stay inside these ranges and needn't reach their ends.
Inputs may be any that keep to these rules, and one draw needn't show every extreme that they name: `fwd_routes`: each row names 8 different experts. For each expert below 4, the 64 rows of one device name it at most 8 times; in every section some expert below 4 is named exactly 8 times by the rows of every device. `bwd_routes`: as for fwd_routes.
All inputs are finite; a program needn't handle non-finite values.
Results may differ from the reference program's by a relative error of at most 0.015.
Values may be sent and summed in bfloat16 or wider, within the bound.
A program may use at most 64 MiB of HBM per device.

```python
import jax
import jax.numpy as jnp
from jax import lax

D = 3584
FF = 1024
EXPERTS = 256
TOPK = 8
SLICES = 8
CAP = 8
TOK_DEV = 64
H_DEV = 128
EXP_FLIGHT = 4
SECTIONS = 16
TOKENS = 2048
N_EXPERT = 32


def route_table(key):
    blocks = TOKENS // TOK_DEV
    subkeys = jax.random.split(key, 5)
    first_draw = jax.random.randint(subkeys[0], (SECTIONS, blocks, EXP_FLIGHT), 0, CAP + 1)
    second_draw = jax.random.randint(subkeys[1], (SECTIONS, blocks, EXP_FLIGHT), 0, CAP + 1)
    row_loads = first_draw * second_draw // CAP
    forced = jnp.arange(EXP_FLIGHT)[None, None, :] == (jnp.arange(SECTIONS) % EXP_FLIGHT)[:, None, None]
    row_loads = jnp.where(forced, CAP, row_loads)
    order_keys = jax.random.randint(subkeys[2], (SECTIONS, blocks, EXP_FLIGHT, TOK_DEV), 0, 2 ** 20) * TOK_DEV + jnp.arange(TOK_DEV)
    row_ranks = jnp.argsort(jnp.argsort(order_keys, axis=-1, stable=True), axis=-1, stable=True)
    member = jnp.transpose(row_ranks < row_loads[..., None], (0, 1, 3, 2))
    other_keys = jax.random.randint(subkeys[3], (SECTIONS, blocks, TOK_DEV, EXPERTS), 0, 2 ** 20) * EXPERTS + jnp.arange(EXPERTS)
    other_keys = jnp.where(jnp.arange(EXPERTS) < EXP_FLIGHT, -1, other_keys)
    others = lax.top_k(other_keys, TOPK)[1].astype(jnp.int32)
    flight_ids = jnp.broadcast_to(jnp.arange(EXP_FLIGHT, dtype=jnp.int32), member.shape)
    candidates = jnp.concatenate([flight_ids, others], axis=-1)
    sort_keys = jnp.concatenate([jnp.where(member, 0, 2 * TOPK + 2), jnp.broadcast_to(jnp.arange(1, TOPK + 1), others.shape)], axis=-1)
    picked = jnp.take_along_axis(candidates, jnp.argsort(sort_keys, axis=-1, stable=True)[..., :TOPK], axis=-1)
    shuffle_keys = jax.random.randint(subkeys[4], picked.shape, 0, 2 ** 20) * TOPK + jnp.arange(TOPK)
    picked = jnp.take_along_axis(picked, jnp.argsort(shuffle_keys, axis=-1, stable=True), axis=-1)
    return picked.reshape(SECTIONS, TOKENS, TOPK).astype(jnp.int32)


def draw_fwd_routes(key, part):
    key = jax.random.fold_in(key, 11)
    return route_table(key)


def draw_bwd_routes(key, part):
    key = jax.random.fold_in(key, 23)
    return route_table(key)


def level_of(rng, dims, cuts, smallest, high):
    loudness = 1.0
    for dim, blocks in cuts:
        steps = jax.random.uniform(jax.random.fold_in(jax.random.fold_in(rng, 6), dim), (blocks,), jnp.float32, smallest / len(cuts), high / len(cuts))
        loudness = loudness * jnp.repeat(jnp.exp(steps), dims[dim] // blocks).reshape((-1,) + (1,) * (len(dims) - 1 - dim))
    return loudness


def gaussian(rng, shape, width, reach, cuts=(), kind=jnp.bfloat16):
    values = jax.random.normal(rng, shape, jnp.float32) * width
    if len(cuts) > 0:
        values = level_of(rng, shape, cuts, -0.22, 0.18) * values
    return jnp.clip(values, min=-reach, max=reach).astype(kind)


def setup_inputs(seed: int = 0) -> dict:
    keys = jax.random.split(jax.random.key(seed), 9)
    return {
        "fwd_tokens": gaussian(keys[0], (SECTIONS, TOKENS, D), 1.0, 6.0, ((0, 16), (1, 32))),
        "bwd_tokens": gaussian(keys[1], (SECTIONS, TOKENS, D), 1.0, 6.0, ((0, 16), (1, 32))),
        "bwd_cotangent": gaussian(keys[2], (SECTIONS, TOKENS, D), 1.0, 6.0, ((0, 16), (1, 32))),
        "fwd_routes": draw_fwd_routes(jax.random.fold_in(keys[8], 71), 0),
        "bwd_routes": draw_bwd_routes(jax.random.fold_in(keys[8], 71), 0),
        "router_weight": gaussian(keys[5], (SECTIONS, D, EXPERTS), D ** -0.5, 0.09375, ((0, 16), (1, 32))),
        "up_weight": gaussian(keys[6], (SECTIONS, D, EXP_FLIGHT * FF), D ** -0.5, 0.09375, ((0, 16), (2, 32))),
        "down_weight": gaussian(keys[7], (SECTIONS, EXP_FLIGHT * FF, D), FF ** -0.5, 0.1875, ((0, 16), (1, 32))),
    }


route_scale = 2.5
highest = lax.Precision.HIGHEST


def silu_slope(values):
    logistic = jax.nn.sigmoid(values)
    return logistic * (1.0 + values * (1.0 - logistic))


def routed_gates(token_rows, routes, router_weight):
    logits = jnp.dot(token_rows, router_weight, preferred_element_type=jnp.float32)
    scores = jax.nn.sigmoid(logits)
    chosen = jnp.take_along_axis(scores, routes, axis=1)
    score_sum = jnp.sum(chosen, axis=1, keepdims=True)
    return scores, chosen, score_sum, route_scale * chosen / score_sum


def expert_rows(routes, expert):
    member = jnp.any(routes == expert, axis=1)
    slot_count = CAP * N_EXPERT
    row_index = jnp.nonzero(member, size=slot_count, fill_value=0)[0].astype(jnp.int32)
    is_live = (jnp.arange(slot_count) < jnp.sum(member.astype(jnp.int32))).astype(jnp.float32)
    return row_index, is_live


def section_layer(fwd_tokens, bwd_tokens, bwd_cotangent, fwd_routes, bwd_routes, router_weight, up_weight, down_weight):
    token_count, model_width = fwd_tokens.shape
    gate_fwd = routed_gates(fwd_tokens, fwd_routes, router_weight)[3]
    scores_bwd, chosen_bwd, score_sum, gate_bwd = routed_gates(bwd_tokens, bwd_routes, router_weight)
    layer_fwd = jnp.zeros((token_count, model_width), jnp.float32)
    input_grad = jnp.zeros((token_count, model_width), jnp.float32)
    gate_grad = jnp.zeros((token_count, TOPK), jnp.float32)
    for expert in range(EXP_FLIGHT):
        up_cols = up_weight[:, expert * FF:(expert + 1) * FF]
        down_rows = down_weight[expert * FF:(expert + 1) * FF, :]
        up_split = up_cols.reshape(model_width, SLICES, H_DEV).astype(jnp.float32)
        down_split = down_rows.reshape(SLICES, H_DEV, model_width).astype(jnp.float32)

        row_index, is_live = expert_rows(fwd_routes, expert)
        picked = fwd_tokens[row_index]
        pre_act = jnp.dot(picked, up_cols, preferred_element_type=jnp.float32)
        activation = jax.nn.silu(pre_act).astype(jnp.bfloat16)
        part_rows = jnp.einsum("nsh,shd->nsd", activation.reshape(-1, SLICES, H_DEV).astype(jnp.float32), down_split, precision=highest)
        part_rows = lax.optimization_barrier(part_rows.astype(jnp.bfloat16))
        output = jnp.sum(part_rows.astype(jnp.float32), axis=1)
        weight = jnp.sum(gate_fwd * (fwd_routes == expert), axis=1)[row_index] * is_live
        layer_fwd = layer_fwd.at[row_index].add(weight[:, None] * output)

        row_index, is_live = expert_rows(bwd_routes, expert)
        picked = bwd_tokens[row_index]
        incoming = bwd_cotangent[row_index]
        pre_act = jnp.dot(picked, up_cols, preferred_element_type=jnp.float32)
        activation = jax.nn.silu(pre_act).astype(jnp.bfloat16)
        part_rows = jnp.einsum("nsh,shd->nsd", activation.reshape(-1, SLICES, H_DEV).astype(jnp.float32), down_split, precision=highest)
        part_rows = lax.optimization_barrier(part_rows.astype(jnp.bfloat16))
        slice_dot = jnp.einsum("nd,nsd->ns", incoming.astype(jnp.float32), part_rows.astype(jnp.float32), precision=highest)
        slice_dot = lax.optimization_barrier(slice_dot.astype(jnp.bfloat16))
        row_dots = jnp.sum(slice_dot.astype(jnp.float32), axis=1) * is_live
        token_dots = jnp.zeros((token_count,), jnp.float32).at[row_index].add(row_dots)
        gate_grad = gate_grad + (bwd_routes == expert).astype(jnp.float32) * token_dots[:, None]
        act_grad = jnp.dot(incoming, down_rows.T, preferred_element_type=jnp.float32)
        pre_grad = (act_grad * silu_slope(pre_act)).astype(jnp.bfloat16)
        grad_rows = jnp.einsum("nsh,dsh->nsd", pre_grad.reshape(-1, SLICES, H_DEV).astype(jnp.float32), up_split, precision=highest)
        grad_rows = lax.optimization_barrier(grad_rows.astype(jnp.bfloat16))
        expert_grad = jnp.sum(grad_rows.astype(jnp.float32), axis=1)
        weight = jnp.sum(gate_bwd * (bwd_routes == expert), axis=1)[row_index] * is_live
        input_grad = input_grad.at[row_index].add(weight[:, None] * expert_grad)
    weighted = jnp.sum(gate_grad * chosen_bwd, axis=1, keepdims=True) / score_sum
    pick_grad = route_scale / score_sum * (gate_grad - weighted)
    one_hot = (bwd_routes[:, :, None] == jnp.arange(router_weight.shape[1])[None, None, :]).astype(jnp.float32)
    score_grad = jnp.sum(one_hot * pick_grad[:, :, None], axis=1)
    logit_grad = (score_grad * scores_bwd * (1.0 - scores_bwd)).astype(jnp.bfloat16)
    router_term = lax.dot_general(logit_grad, router_weight, (((1,), (1,)), ((), ())), preferred_element_type=jnp.float32)
    layer_bwd = (input_grad + router_term).astype(jnp.bfloat16)
    return layer_fwd.astype(jnp.bfloat16), layer_bwd


def reference(fwd_tokens, bwd_tokens, bwd_cotangent, fwd_routes, bwd_routes, router_weight, up_weight, down_weight):
    def one_section(section_items):
        return section_layer(section_items[0], section_items[1], section_items[2], section_items[3], section_items[4], section_items[5], section_items[6], section_items[7])

    layer_fwd, layer_bwd = lax.map(one_section, (fwd_tokens, bwd_tokens, bwd_cotangent, fwd_routes, bwd_routes, router_weight, up_weight, down_weight))
    return jnp.roll(layer_fwd, 1, axis=0), jnp.roll(layer_bwd, 1, axis=0)
```

```python
import functools

import jax
import jax.numpy as jnp
from jax import lax
from jax.experimental import pallas as pl
from jax.experimental.pallas import tpu as pltpu
from jax.sharding import PartitionSpec as P

MESH = pl.DeviceIdType.MESH
D = 3584
HALF = D // 2
EXPERTS = 256
CAP = 8
FLIGHT = 4
SLOTS = FLIGHT * CAP
TOK = 64
HID = 128
WROWS = 112
NY = 8
SECTIONS = 16
ROUTE_SCALE = 2.5
HIGHEST = lax.Precision.HIGHEST
F32 = jnp.float32
BF16 = jnp.bfloat16
OFFSETS = (2, -1, -3)


def across(a, b):
    return lax.dot_general(a, b, (((1,), (1,)), ((), ())), preferred_element_type=F32)


def dot(a, b):
    return jnp.dot(a, b, preferred_element_type=F32)


def exact(a, b):
    return jnp.dot(a, b, preferred_element_type=F32, precision=HIGHEST)


def sigmoid(v):
    return 1.0 / (1.0 + jnp.exp(-v))


def chosen_mask(routes_ref):
    ids = lax.broadcasted_iota(jnp.int32, (TOK, EXPERTS), 1)
    mask = jnp.zeros((TOK, EXPERTS), F32)
    for k in range(routes_ref.shape[1]):
        mask = mask + jnp.where(routes_ref[:, k : k + 1] == ids, 1.0, 0.0)
    return mask


def to_slots(columns):
    lane = lax.broadcasted_iota(jnp.int32, (TOK, 128), 1)
    out = jnp.zeros((TOK, 128), F32)
    for e in range(FLIGHT):
        inside = (lane >= e * CAP) & (lane < (e + 1) * CAP)
        out = out + jnp.where(inside, jnp.broadcast_to(columns[:, e : e + 1], (TOK, 128)), 0.0)
    return out


def slot_select(mask):
    member = to_slots(mask)
    row = lax.broadcasted_iota(jnp.int32, (TOK, TOK), 0)
    col = lax.broadcasted_iota(jnp.int32, (TOK, TOK), 1)
    below = jnp.where(col < row, 1.0, 0.0).astype(BF16)
    placing = dot(below, member.astype(BF16))
    lane = lax.broadcasted_iota(jnp.int32, (TOK, 128), 1)
    slot = (lane % CAP).astype(F32)
    return jnp.where(placing == slot, member, 0.0)


def kernel(
    xf_hbm, xb_hbm, g_hbm, rf_ref, rb_ref, w_hbm, up_hbm, dn_hbm,
    of_ref, ob_ref,
    xf, xb, g, up, dn, wg, pb, pf, pfx, rows_b, rows_f,
    acc1, acc2, send_dot, got_dot, out_b, out_f, rx_b, rx_f,
    ps_b, ps_f, pr_b, pr_f, fs_b, fs_f, fin_b, fin_f,
    msg, msg_in, rr, rr_in,
    lsem, ssem, rsem,
):
    p = lax.axis_index("pipe")
    me = lax.axis_index("expert")
    y = me // 4
    xh = (me // 2) % 2
    c = me % 2
    e = y // 2
    sig = 1 - 2 * (y % 2)
    nxt = (p + 1) % SECTIONS
    prv = (p + SECTIONS - 1) % SECTIONS

    def at(yy, xx=None, cc=None, pp=None):
        xx = xh if xx is None else xx
        cc = c if cc is None else cc
        return (p if pp is None else pp, (yy * 2 + xx) * 2 + cc)

    def shift(off):
        return (y + NY + sig * off) % NY

    def slot_y(s):
        return shift(-s) if s < 4 else shift(s - 3)

    sib = at(y, cc=1 - c)
    xpart = at(y, xx=1 - xh)
    pair = at(shift(1))

    bar = pltpu.get_barrier_semaphore()

    def greet(dev):
        pl.semaphore_signal(bar, inc=1, device_id=dev, device_id_type=MESH)

    for s in range(8):
        if s:
            greet(at(slot_y(s)))
        greet(at(slot_y(s), xx=1 - xh))
    greet(sib)
    greet(at(y, pp=prv))
    greet(at(y, xx=1 - xh, pp=prv))

    nsem = [0]
    nlocal = [0]
    sends = []

    def ids(n):
        first = nsem[0]
        nsem[0] += n
        return first

    def local(src, dst):
        cp = pltpu.make_async_copy(src, dst, lsem.at[nlocal[0]])
        nlocal[0] += 1
        cp.start()
        return cp

    def push(src, dst, dev, s_id, r_id=None):
        cp = pltpu.make_async_remote_copy(
            src_ref=src, dst_ref=dst, send_sem=ssem.at[s_id],
            recv_sem=rsem.at[s_id if r_id is None else r_id],
            device_id=dev, device_id_type=MESH,
        )
        cp.start()
        sends.append(cp)

    def got(dst, r_id):
        pltpu.make_async_remote_copy(
            src_ref=dst, dst_ref=dst, send_sem=ssem.at[0], recv_sem=rsem.at[r_id],
            device_id=sib, device_id_type=MESH,
        ).wait_recv()

    l_xb = local(xb_hbm, xb)
    l_g = local(g_hbm, g)
    l_xf = local(xf_hbm, xf)
    l_up = local(up_hbm, up.at[:, pl.ds(0, HID)])
    l_dn = local(dn_hbm, dn.at[pl.ds(0, HID)])
    my_w = y * 2 + xh
    l_w = local(w_hbm, wg.at[my_w, c])

    mask_b = chosen_mask(rb_ref)
    mask_f = chosen_mask(rf_ref)
    sel_b = slot_select(mask_b)
    sel_f = slot_select(mask_f)
    pick_b = sel_b.T[:SLOTS].astype(BF16)
    pick_f = sel_f.T[:SLOTS].astype(BF16)

    l_xb.wait()
    l_g.wait()

    @pl.loop(0, 7)
    def _(i):
        cols = pl.ds(pl.multiple_of(i * 512, 512), 512)
        a = dot(pick_b, xb[:, cols]).reshape(FLIGHT, CAP, 512)
        b = dot(pick_b, g[:, cols]).reshape(FLIGHT, CAP, 512)
        pb[:, :, cols] = jnp.concatenate([a, b], axis=1).astype(BF16)

    l_xf.wait()

    @pl.loop(0, 7)
    def _(i):
        lo = pl.ds(pl.multiple_of(i * 256, 256), 256)
        hi = pl.ds(pl.multiple_of(HALF + i * 256, 256), 256)
        a = dot(pick_f, xf[:, lo]).reshape(FLIGHT, CAP, 256)
        b = dot(pick_f, xf[:, hi]).reshape(FLIGHT, CAP, 256)
        pf[:, :, lo] = jnp.concatenate([a, b], axis=1).astype(BF16)

    pl.semaphore_wait(bar, 18)

    by = ids(8)
    bx = ids(8)
    for off in OFFSETS:
        t = shift(off)
        push(pb.at[t // 2], rows_b.at[0, abs(off)], at(t), by + abs(off))
    push(pb.at[e], rows_b.at[0, 4], pair, by + 4)
    push(pb.at[e], rows_b.at[1, 0], xpart, bx)
    l_b0 = local(pb.at[e], rows_b.at[0, 0])

    fx = ids(1)
    push(pf, pfx, xpart, fx)

    su = ids(2)
    push(up_hbm, up.at[:, pl.ds(HID, HID)], sib, su)
    push(dn_hbm, dn.at[pl.ds(HID, HID)], sib, su + 1)
    wx = ids(1)
    push(w_hbm, wg.at[my_w, c], xpart, wx)

    fy = [ids(8), ids(8)]

    def send_f(col, src):
        for off in OFFSETS:
            t = shift(off)
            push(src.at[t // 2], rows_f.at[col, abs(off)], at(t), fy[col] + abs(off))
        push(src.at[e], rows_f.at[col, 4], pair, fy[col] + 4)
        return local(src.at[e], rows_f.at[col, 0])

    def hand_b(s):
        got(rows_b.at[0, s], by + s)
        if s < 4:
            push(rows_b.at[0, s], rows_b.at[0, 4 + s], pair, by + 4 + s)
        push(rows_b.at[0, s], rows_b.at[1, s], xpart, bx + s)

    def hand_f(col, s):
        got(rows_f.at[col, s], fy[col] + s)
        push(rows_f.at[col, s], rows_f.at[col, 4 + s], pair, fy[col] + 4 + s)

    l_f0 = send_f(0, pf)
    hand_b(1)
    hand_b(4)
    got(pfx, fx)
    l_f1 = send_f(1, pfx)
    for s in (2, 5, 3, 6, 7):
        hand_b(s)
    for s in (1, 2, 3):
        hand_f(0, s)
        hand_f(1, s)

    up_dev, down_dev = at((y + 1) % NY), at((y + NY - 1) % NY)
    wr = ids(16)
    l_w.wait()
    got(wg.at[y * 2 + (1 - xh), c], wx)

    def ring(step):
        yu = (y + NY - step) % NY
        yd = (y + step) % NY
        for xx in range(2):
            if step < 3 or xx == 0:
                push(wg.at[yu * 2 + xx, c], wg.at[yu * 2 + xx, c], up_dev, wr + step * 2 + xx)
            if step < 3 or xx == 1:
                push(wg.at[yd * 2 + xx, c], wg.at[yd * 2 + xx, c], down_dev, wr + 8 + step * 2 + xx)

    def ring_got(step):
        yu = (y + NY - step - 1) % NY
        yd = (y + step + 1) % NY
        for xx in range(2):
            if step < 3 or xx == 0:
                got(wg.at[yu * 2 + xx, c], wr + step * 2 + xx)
            if step < 3 or xx == 1:
                got(wg.at[yd * 2 + xx, c], wr + 8 + step * 2 + xx)

    ring(0)

    l_b0.wait()
    l_up.wait()
    l_dn.wait()
    got(up.at[:, pl.ds(HID, HID)], su)
    got(dn.at[pl.ds(HID, HID)], su + 1)
    for s in range(8):
        got(rows_b.at[1, s], bx + s)

    acc1[...] = jnp.zeros_like(acc1)
    acc2[...] = jnp.zeros_like(acc2)

    @pl.loop(0, 7)
    def _(i):
        cols = pl.ds(pl.multiple_of(i * 512, 512), 512)
        r = rows_b[:, :, :, cols].reshape(256, 512)
        acc1[...] += dot(r, up[cols, :])
        acc2[...] += across(r, dn[:, cols])

    pre = acc1[...].reshape(16, 16, 256)[:, :CAP].reshape(128, 256)
    act_grad = acc2[...].reshape(16, 16, 256)[:, CAP:].reshape(128, 256)
    s = sigmoid(pre)
    act = (pre * s).astype(BF16).astype(F32)
    dots = jnp.sum(act * act_grad, axis=1, keepdims=True)
    send_dot[...] = jnp.broadcast_to(dots, (128, 128)).reshape(2, 8, CAP, 128)
    mine = e * 4 + (y % 2) * 2 + xh
    dt_s = ids(16)
    dt_r = ids(16)
    for col in range(2):
        for k in range(8):
            if col == 0 and k == 0:
                continue
            dev = at(slot_y(k), xx=xh if col == 0 else 1 - xh)
            push(send_dot.at[col, k], got_dot.at[mine], dev, dt_s + col * 8 + k, dt_r + mine)
    l_dot = local(send_dot.at[0, 0], got_dot.at[mine])

    pre_grad = (act_grad * (s * (1.0 + pre * (1.0 - s)))).astype(BF16)

    @pl.loop(0, 7)
    def _(i):
        lo = pl.ds(pl.multiple_of(i * 256, 256), 256)
        hi = pl.ds(pl.multiple_of(HALF + i * 256, 256), 256)
        a = across(pre_grad, up[lo, :]).reshape(2, 8, CAP, 256)
        b = across(pre_grad, up[hi, :]).reshape(2, 8, CAP, 256)
        out_b[:, :, :, lo] = jnp.concatenate([a, b], axis=2).astype(BF16)

    def send_back(out, rx, first):
        for half in (1, 0):
            part = pl.ds(half * 4, 4)
            for col in range(2):
                dev = at(y, xx=xh if col == 0 else 1 - xh, pp=nxt)
                push(out.at[col, part], rx.at[col, part], dev, first + half * 2 + col)

    rb = ids(4)
    send_back(out_b, rx_b, rb)
    ring_got(0)
    ring(1)

    l_f0.wait()
    l_f1.wait()
    for col in range(2):
        for k in range(4, 8):
            got(rows_f.at[col, k], fy[col] + k)
    acc1[...] = jnp.zeros_like(acc1)
    acc2[...] = jnp.zeros_like(acc2)

    @pl.loop(0, 7)
    def _(i):
        lo = pl.ds(pl.multiple_of(i * 256, 256), 256)
        hi = pl.ds(pl.multiple_of(HALF + i * 256, 256), 256)
        r = rows_f[:, :, :, lo].reshape(256, 256)
        acc1[...] += dot(r, up[lo, :])
        acc2[...] += dot(r, up[hi, :])

    pre_f = (
        acc1[...].reshape(16, 16, 256)[:, :CAP] + acc2[...].reshape(16, 16, 256)[:, CAP:]
    ).reshape(128, 256)
    act_f = (pre_f * sigmoid(pre_f)).astype(BF16)

    @pl.loop(0, 7)
    def _(i):
        lo = pl.ds(pl.multiple_of(i * 256, 256), 256)
        hi = pl.ds(pl.multiple_of(HALF + i * 256, 256), 256)
        a = dot(act_f, dn[:, lo]).reshape(2, 8, CAP, 256)
        b = dot(act_f, dn[:, hi]).reshape(2, 8, CAP, 256)
        out_f[:, :, :, lo] = jnp.concatenate([a, b], axis=2).astype(BF16)

    rf = ids(4)
    send_back(out_f, rx_f, rf)
    ring_got(1)
    ring(2)

    def to_pair(rx, ps, pr, first, pid):
        got(rx.at[0, pl.ds(4, 4)], first + 2)
        got(rx.at[1, pl.ds(4, 4)], first + 3)

        @pl.loop(0, 4)
        def _(k):
            ps[k] = (rx[0, 4 + k].astype(F32) + rx[1, 4 + k].astype(F32)).astype(BF16)

        push(ps, pr, pair, pid)

    def to_home(rx, pr, fs, fin, first, pid, s_id, r_id):
        got(rx.at[0, pl.ds(0, 4)], first)
        got(rx.at[1, pl.ds(0, 4)], first + 1)
        got(pr, pid)

        @pl.loop(0, 4)
        def _(k):
            fs[k] = (rx[0, k].astype(F32) + rx[1, k].astype(F32) + pr[k].astype(F32)).astype(BF16)

        for k in range(1, 4):
            push(fs.at[k], fin.at[e], at(shift(-k)), s_id + k, r_id + e)
        return local(fs.at[0], fin.at[e])

    pid_b, pid_f = ids(1), ids(1)
    hs_b, hr_b, hs_f, hr_f = ids(4), ids(4), ids(4), ids(4)
    to_pair(rx_b, ps_b, pr_b, rb, pid_b)
    ring_got(2)
    ring(3)
    l_hb = to_home(rx_b, pr_b, fs_b, fin_b, rb, pid_b, hs_b, hr_b)
    ring_got(3)
    ws = ids(1)
    push(wg.at[:, c], wg.at[:, c], sib, ws)
    to_pair(rx_f, ps_f, pr_f, rf, pid_f)
    got(wg.at[:, 1 - c], ws)

    def scores(x):
        total = jnp.zeros((TOK, EXPERTS), F32)
        for i in range(4):
            w = wg[pl.ds(4 * i, 4)].reshape(896, EXPERTS)
            total = total + dot(x[:, pl.ds(896 * i, 896)], w)
        return sigmoid(total)

    score_f = scores(xf)
    score_b = scores(xb)
    sum_f = jnp.sum(mask_f * score_f, axis=1, keepdims=True)
    sum_b = jnp.sum(mask_b * score_b, axis=1, keepdims=True)
    msg[0] = sel_f * to_slots(ROUTE_SCALE * score_f / sum_f)
    msg[1] = sel_b * to_slots(ROUTE_SCALE * score_b / sum_b)
    seen = jnp.zeros((TOK, 1), F32)
    firsts = []
    for k in range(FLIGHT):
        here = mask_b[:, k : k + 1]
        firsts.append(here * (1.0 - seen))
        seen = jnp.maximum(seen, here)
    lane = lax.broadcasted_iota(jnp.int32, (TOK, 128), 1)
    first = jnp.zeros((TOK, 128), F32)
    for k in range(FLIGHT):
        inside = (lane >= k * CAP) & (lane < (k + 1) * CAP)
        first = first + jnp.where(inside, jnp.broadcast_to(firsts[k], (TOK, 128)), 0.0)
    once = sel_b * first
    msg[2] = once
    mg = ids(1)
    push(msg, msg_in, at(y, pp=nxt), mg)

    l_dot.wait()
    for k in range(1, 16):
        other = (mine + k) % 16
        got(got_dot.at[other], dt_r + other)
    all_dots = got_dot[...].reshape(FLIGHT, 4, CAP, 128)
    slot_dots = (all_dots[:, 0] + all_dots[:, 1] + all_dots[:, 2] + all_dots[:, 3]).reshape(SLOTS, 128)
    slot_row = lax.broadcasted_iota(jnp.int32, (SLOTS, EXPERTS), 0)
    slot_col = lax.broadcasted_iota(jnp.int32, (SLOTS, EXPERTS), 1)
    by_expert = jnp.where(
        slot_row // CAP == slot_col, jnp.broadcast_to(slot_dots[:, 0:1], (SLOTS, EXPERTS)), 0.0
    )
    gate_grad = exact(sel_b[:, :SLOTS], by_expert)
    weighted = jnp.sum(gate_grad * score_b, axis=1, keepdims=True) / sum_b
    pick_grad = ROUTE_SCALE / sum_b * (gate_grad - weighted)
    logit_grad = (mask_b * pick_grad * score_b * (1.0 - score_b)).astype(BF16)
    packed = dot(once.T[:SLOTS].astype(BF16), logit_grad).astype(BF16)
    for i in range(4):
        w = wg[pl.ds(4 * i, 4)].reshape(896, EXPERTS)
        rr[:, pl.ds(896 * i, 896)] = across(packed, w).astype(BF16)
    rid = ids(1)
    push(rr, rr_in, at(y, pp=nxt), rid)

    l_hf = to_home(rx_f, pr_f, fs_f, fin_f, rf, pid_f, hs_f, hr_f)

    got(msg_in, mg)
    l_hb.wait()
    for k in range(1, 4):
        got(fin_b.at[(e + k) % 4], hr_b + (e + k) % 4)
    got(rr_in, rid)
    gate_b = msg_in[1][:, :SLOTS]
    once_in = msg_in[2][:, :SLOTS].astype(BF16)

    @pl.loop(0, 7)
    def _(i):
        lo = pl.ds(pl.multiple_of(i * 256, 256), 256)
        hi = pl.ds(pl.multiple_of(HALF + i * 256, 256), 256)
        t = fin_b[:, :, lo].astype(F32)
        a = exact(gate_b, t[:, :CAP].reshape(SLOTS, 256)) + dot(once_in, rr_in[:, lo])
        b = exact(gate_b, t[:, CAP:].reshape(SLOTS, 256)) + dot(once_in, rr_in[:, hi])
        ob_ref[:, lo] = a.astype(BF16)
        ob_ref[:, hi] = b.astype(BF16)

    l_hf.wait()
    for k in range(1, 4):
        got(fin_f.at[(e + k) % 4], hr_f + (e + k) % 4)
    gate_f = msg_in[0][:, :SLOTS]

    @pl.loop(0, 7)
    def _(i):
        lo = pl.ds(pl.multiple_of(i * 256, 256), 256)
        hi = pl.ds(pl.multiple_of(HALF + i * 256, 256), 256)
        t = fin_f[:, :, lo].astype(F32)
        of_ref[:, lo] = exact(gate_f, t[:, :CAP].reshape(SLOTS, 256)).astype(BF16)
        of_ref[:, hi] = exact(gate_f, t[:, CAP:].reshape(SLOTS, 256)).astype(BF16)

    for cp in sends:
        cp.wait_send()


N_SEM = 160


def on_device(xf, xb, g, rf, rb, w, up, dn):
    vm = pltpu.VMEM
    scratch = [
        vm((TOK, D), BF16), vm((TOK, D), BF16), vm((TOK, D), BF16),
        vm((D, 2 * HID), BF16), vm((2 * HID, D), BF16), vm((16, 2, WROWS, EXPERTS), BF16),
        vm((FLIGHT, 16, D), BF16), vm((FLIGHT, 16, HALF), BF16), vm((FLIGHT, 16, HALF), BF16),
        vm((2, 8, 16, D), BF16), vm((2, 8, 16, HALF), BF16),
        vm((256, 256), F32), vm((256, 256), F32),
        vm((2, 8, CAP, 128), F32), vm((16, CAP, 128), F32),
        vm((2, 8, 16, HALF), BF16), vm((2, 8, 16, HALF), BF16),
        vm((2, 8, 16, HALF), BF16), vm((2, 8, 16, HALF), BF16),
        vm((4, 16, HALF), BF16), vm((4, 16, HALF), BF16),
        vm((4, 16, HALF), BF16), vm((4, 16, HALF), BF16),
        vm((4, 16, HALF), BF16), vm((4, 16, HALF), BF16),
        vm((4, 16, HALF), BF16), vm((4, 16, HALF), BF16),
        vm((3, TOK, 128), F32), vm((3, TOK, 128), F32),
        vm((SLOTS, D), BF16), vm((SLOTS, D), BF16),
        pltpu.SemaphoreType.DMA((16,)),
        pltpu.SemaphoreType.DMA((N_SEM,)),
        pltpu.SemaphoreType.DMA((N_SEM,)),
    ]
    hbm = pl.BlockSpec(memory_space=pl.ANY)
    vmem = pl.BlockSpec(memory_space=pltpu.VMEM)
    of, ob = pl.pallas_call(
        kernel,
        out_shape=[jax.ShapeDtypeStruct((TOK, D), BF16)] * 2,
        in_specs=[hbm, hbm, hbm, vmem, vmem, hbm, hbm, hbm],
        out_specs=[vmem, vmem],
        scratch_shapes=scratch,
        compiler_params=pltpu.CompilerParams(
            collective_id=0, has_side_effects=True, vmem_limit_bytes=60 * 2**20
        ),
        cost_estimate=pl.CostEstimate(flops=2 * 10**9, bytes_accessed=6 * 10**6, transcendentals=10**5),
        name="expert_layer",
    )(xf[0], xb[0], g[0], rf[0], rb[0], w[0], up[0], dn[0])
    return of[None], ob[None]


def solution(mesh):
    rows = P("pipe", "expert", None)
    return jax.shard_map(
        on_device,
        mesh=mesh,
        in_specs=(rows, rows, rows, rows, rows, rows, P("pipe", None, "expert"), rows),
        out_specs=(rows, rows),
        check_vma=False,
    )
```

```python
import functools

import jax
import jax.numpy as jnp
from jax import lax
from jax.experimental import pallas as pl
from jax.experimental.pallas import tpu as pltpu
from jax.sharding import PartitionSpec as P

MESH = pl.DeviceIdType.MESH
D = 3584
HALF = D // 2
PART = HALF // 2
EXPERTS = 256
CAP = 8
FLIGHT = 4
SLOTS = FLIGHT * CAP
TOK = 64
HID = 128
WROWS = 112
NY = 8
DN = 4
SECTIONS = 16
ROUTE_SCALE = 2.5
HIGHEST = lax.Precision.HIGHEST
F32 = jnp.float32
BF16 = jnp.bfloat16
OFFSETS = (-1, 2, -3)


def across(a, b):
    return lax.dot_general(a, b, (((1,), (1,)), ((), ())), preferred_element_type=F32)


def dot(a, b):
    return jnp.dot(a, b, preferred_element_type=F32)


def exact(a, b):
    return jnp.dot(a, b, preferred_element_type=F32, precision=HIGHEST)


def sigmoid(v):
    return 1.0 / (1.0 + jnp.exp(-v))


def chosen_mask(routes_ref):
    wide = jnp.concatenate([routes_ref[...].astype(F32)] * 2, axis=1)
    routes = wide.T[:TOK]
    ids = lax.broadcasted_iota(jnp.int32, (TOK, EXPERTS), 1).astype(F32)
    mask = jnp.zeros((TOK, EXPERTS), F32)
    for k in range(routes_ref.shape[0]):
        mask = mask + jnp.where(routes[:, k : k + 1] == ids, 1.0, 0.0)
    return mask


def two_parts(v):
    high = v.astype(BF16)
    return high, (v - high.astype(F32)).astype(BF16)


def to_slots(columns):
    lane = lax.broadcasted_iota(jnp.int32, (TOK, 128), 1)
    out = jnp.zeros((TOK, 128), F32)
    for e in range(FLIGHT):
        inside = (lane >= e * CAP) & (lane < (e + 1) * CAP)
        out = out + jnp.where(inside, jnp.broadcast_to(columns[:, e : e + 1], (TOK, 128)), 0.0)
    return out


def slot_select(mask):
    member = to_slots(mask)
    row = lax.broadcasted_iota(jnp.int32, (TOK, TOK), 0)
    col = lax.broadcasted_iota(jnp.int32, (TOK, TOK), 1)
    below = jnp.where(col < row, 1.0, 0.0).astype(BF16)
    placing = dot(below, member.astype(BF16))
    lane = lax.broadcasted_iota(jnp.int32, (TOK, 128), 1)
    slot = (lane % CAP).astype(F32)
    return jnp.where(placing == slot, member, 0.0)


def kernel(
    xf_hbm, xb_hbm, g_hbm, rf_ref, rb_ref, w_hbm, up_hbm, dn_hbm,
    of_ref, ob_ref,
    xf, xb, g, up, dn, wg, pb, pf, rows_b, rows_f,
    pre_b, grad_b, pre_f, send_dot, got_dot, out_b, out_f,
    pr_b, pr_f, fs_b, fs_f, fin_b, fin_f,
    msg, msg_in, lg, lg_in,
    lsem, ssem, rsem,
):
    p = lax.axis_index("pipe")
    me = lax.axis_index("expert")
    y = me // 4
    xh = (me // 2) % 2
    c = me % 2
    e = y // 2
    sig = 1 - 2 * (y % 2)
    nxt = (p + 1) % SECTIONS
    prv = (p + SECTIONS - 1) % SECTIONS

    def at(yy, xx=None, cc=None, pp=None):
        xx = xh if xx is None else xx
        cc = c if cc is None else cc
        return (p if pp is None else pp, (yy * 2 + xx) * 2 + cc)

    def shift(off):
        return (y + NY + sig * off) % NY

    def slot_y(s):
        return shift(-s) if s < 4 else shift(s - 3)

    sib = at(y, cc=1 - c)
    xpart = at(y, xx=1 - xh)
    pair = at(shift(1))

    bar = pltpu.get_barrier_semaphore()

    def greet(dev):
        pl.semaphore_signal(bar, inc=1, device_id=dev, device_id_type=MESH)

    for s in range(1, 8):
        greet(at(slot_y(s)))
    greet(xpart)
    greet(sib)
    greet(at(y, pp=prv))
    greet(at(y, xx=1 - xh, pp=prv))
    for off in OFFSETS:
        greet(at(shift(off), pp=prv))

    nsem = [0]
    nlocal = [0]
    sends = []

    def ids(n):
        first = nsem[0]
        nsem[0] += n
        return first

    def local(src, dst):
        cp = pltpu.make_async_copy(src, dst, lsem.at[nlocal[0]])
        nlocal[0] += 1
        cp.start()
        return cp

    def push(src, dst, dev, s_id, r_id=None):
        cp = pltpu.make_async_remote_copy(
            src_ref=src, dst_ref=dst, send_sem=ssem.at[s_id],
            recv_sem=rsem.at[s_id if r_id is None else r_id],
            device_id=dev, device_id_type=MESH,
        )
        cp.start()
        sends.append(cp)

    def got(dst, r_id):
        pltpu.make_async_remote_copy(
            src_ref=dst, dst_ref=dst, send_sem=ssem.at[0], recv_sem=rsem.at[r_id],
            device_id=sib, device_id_type=MESH,
        ).wait_recv()

    l_xb = local(xb_hbm, xb)
    l_g = local(g_hbm, g)
    l_xf = local(xf_hbm, xf)
    l_up = local(up_hbm, up.at[:, pl.ds(0, HID)])
    l_dn = local(dn_hbm, dn.at[pl.ds(0, HID)])
    my_w = y * 2 + xh
    l_w = local(w_hbm, wg.at[0, my_w, c])

    mask_b = chosen_mask(rb_ref)
    mask_f = chosen_mask(rf_ref)
    sel_b = slot_select(mask_b)
    sel_f = slot_select(mask_f)
    pick_b = sel_b.T[:SLOTS].astype(BF16)
    pick_f = sel_f.T[:SLOTS].astype(BF16)

    l_xb.wait()
    l_g.wait()
    for i in range(7):
        cols = pl.ds(i * 512, 512)
        a = dot(pick_b, xb[:, cols]).reshape(FLIGHT, CAP, 512)
        b = dot(pick_b, g[:, cols]).reshape(FLIGHT, CAP, 512)
        pb[:, :, cols] = jnp.concatenate([a, b], axis=1).astype(BF16)

    pl.semaphore_wait(bar, 14)

    def up_part(k, rows):
        return up.at[rows, pl.ds(k * HID, HID)]

    def dn_part(k, rows):
        return dn.at[pl.ds(k * HID + rows.start, rows.size)]

    up_rows = [pl.ds(i * HALF, HALF) for i in range(2)]
    dn_rows = [pl.ds(i * (HID // DN), HID // DN) for i in range(DN)]
    ux, us, uy, dx, ds_, dy = ids(2), ids(2), ids(2), ids(DN), ids(DN), ids(DN)

    def enter(src, rows, iy):
        push(src.at[e], rows.at[4], pair, iy + 4)
        for off in OFFSETS:
            t = shift(off)
            push(src.at[t // 2], rows.at[abs(off)], at(t), iy + abs(off))
        return local(src.at[e], rows.at[0])

    def hands(rows, iy, slots):
        for s in slots:
            got(rows.at[s], iy + s)
            push(rows.at[s], rows.at[4 + s], pair, iy + 4 + s)

    iy_b, iy_f = ids(8), ids(8)
    l_b0 = enter(pb, rows_b, iy_b)
    for i in range(2):
        push(up_hbm.at[up_rows[i]], up_part(1, up_rows[i]), sib, us + i)
    for i in range(DN):
        push(dn_hbm.at[dn_rows[i]], dn_part(1, dn_rows[i]), sib, ds_ + i)
    wx = ids(3)
    push(w_hbm, wg.at[0, my_w, c], xpart, wx)
    push(w_hbm, wg.at[1, my_w, c], at(y, pp=nxt), wx + 1)
    push(w_hbm, wg.at[1, my_w, c], at(y, xx=1 - xh, pp=nxt), wx + 2)

    l_xf.wait()
    for i in range(7):
        lo = pl.ds(i * 256, 256)
        hi = pl.ds(HALF + i * 256, 256)
        a = dot(pick_f, xf[:, lo]).reshape(FLIGHT, CAP, 256)
        b = dot(pick_f, xf[:, hi]).reshape(FLIGHT, CAP, 256)
        pf[:, :, lo] = jnp.concatenate([a, b], axis=1).astype(BF16)

    l_f0 = enter(pf, rows_f, iy_f)

    up_dev, down_dev = at((y + 1) % NY), at((y + NY - 1) % NY)
    wr = ids(16)

    def ring(step):
        yu = (y + NY - step) % NY
        yd = (y + step) % NY
        for xx in range(2):
            if step < 3 or xx == 0:
                push(wg.at[:, yu * 2 + xx, c], wg.at[:, yu * 2 + xx, c], up_dev, wr + step * 2 + xx)
            if step < 3 or xx == 1:
                push(wg.at[:, yd * 2 + xx, c], wg.at[:, yd * 2 + xx, c], down_dev, wr + 8 + step * 2 + xx)

    wsib = ids(18)

    def to_sibling(idx, n):
        push(wg.at[:, idx, c], wg.at[:, idx, c], sib, wsib + n)

    def from_sibling(idx, n):
        got(wg.at[:, idx, 1 - c], wsib + n)

    def ring_blocks(step):
        yu = (y + NY - step - 1) % NY
        yd = (y + step + 1) % NY
        for xx in range(2):
            if step < 3 or xx == 0:
                yield yu * 2 + xx, step * 2 + xx
            if step < 3 or xx == 1:
                yield yd * 2 + xx, 8 + step * 2 + xx

    def ring_got(step):
        for idx, n in ring_blocks(step):
            got(wg.at[:, idx, c], wr + n)
            to_sibling(idx, n)

    own, other = pl.ds(0, 2 * HID), pl.ds(2 * HID, 2 * HID)

    def forward_pre(lanes):
        r = rows_f[...].reshape(128, HALF)
        low = dot(r, up[pl.ds(0, HALF), lanes]).reshape(8, 16, 256)[:, :CAP]
        high = dot(r, up[pl.ds(HALF, HALF), lanes]).reshape(8, 16, 256)[:, CAP:]
        pre_f[:, lanes] = (low + high).reshape(64, 256)

    def backward_pre(lanes):
        r = rows_b[...].reshape(128, D)
        pre_b[:, lanes] = dot(r, up[:, lanes]).reshape(8, 16, 256)[:, :CAP].reshape(64, 256)

    def backward_grad(lanes):
        r = rows_b[...].reshape(128, D)
        grad_b[:, lanes] = across(r, dn[lanes, :]).reshape(8, 16, 256)[:, CAP:].reshape(64, 256)


    def up_on(i):
        got(up_part(2, up_rows[i]), ux + i)
        push(up_part(2, up_rows[i]), up_part(3, up_rows[i]), sib, uy + i)

    def dn_on(i):
        got(dn_part(2, dn_rows[i]), dx + i)
        push(dn_part(2, dn_rows[i]), dn_part(3, dn_rows[i]), sib, dy + i)

    def send_up(i):
        push(up_hbm.at[up_rows[i]], up_part(2, up_rows[i]), xpart, ux + i)

    def send_dn(i):
        push(dn_hbm.at[dn_rows[i]], dn_part(2, dn_rows[i]), xpart, dx + i)

    send_up(0)
    send_up(1)
    for i in range(DN):
        send_dn(i)
    hands(rows_b, iy_b, (1,))
    l_w.wait()
    their_w = y * 2 + (1 - xh)
    got(wg.at[0, their_w, c], wx)
    got(wg.at[1, my_w, c], wx + 1)
    got(wg.at[1, their_w, c], wx + 2)
    ring(0)
    to_sibling(my_w, 16)
    to_sibling(their_w, 17)
    hands(rows_b, iy_b, (2, 3))
    hands(rows_f, iy_f, (1, 2, 3))
    ring_got(0)
    ring(1)
    l_b0.wait()
    l_f0.wait()
    l_up.wait()
    l_dn.wait()
    for i in range(2):
        got(up_part(1, up_rows[i]), us + i)
    for i in range(DN):
        got(dn_part(1, dn_rows[i]), ds_ + i)
    for s in range(4, 8):
        got(rows_b.at[s], iy_b + s)
    backward_pre(own)
    backward_grad(own)
    ring_got(1)
    ring(2)
    up_on(0)
    for s in range(4, 8):
        got(rows_f.at[s], iy_f + s)
    forward_pre(own)
    ring_got(2)
    ring(3)
    up_on(1)
    for i in range(2):
        got(up_part(3, up_rows[i]), uy + i)
    backward_pre(other)
    forward_pre(other)
    ring_got(3)
    for i in range(DN):
        dn_on(i)
    for i in range(DN):
        got(dn_part(3, dn_rows[i]), dy + i)
    backward_grad(other)
    pre = pre_b[...]
    act_grad = grad_b[...]
    s = sigmoid(pre)
    act = (pre * s).astype(BF16).astype(F32)
    dots = jnp.sum(act * act_grad, axis=1, keepdims=True)
    send_dot[...] = jnp.broadcast_to(dots, (64, 128)).reshape(8, CAP, 128)
    pre_grad = (act_grad * (s * (1.0 + pre * (1.0 - s)))).astype(BF16)
    back_b, back_f = ids(2), ids(2)
    for i in range(2):
        a = across(pre_grad, up[pl.ds(i * PART, PART), :]).reshape(8, CAP, PART)
        b = across(pre_grad, up[pl.ds(HALF + i * PART, PART), :]).reshape(8, CAP, PART)
        out_b[i] = jnp.concatenate([a, b], axis=1).astype(BF16)
        push(out_b.at[i, pl.ds(4, 4)], pr_b.at[i], pair, back_b + i)
    mine = e * 2 + y % 2
    dt_s, dt_r = ids(8), ids(8)
    for k in range(1, 8):
        push(send_dot.at[k], got_dot.at[mine], at(slot_y(k)), dt_s + k, dt_r + mine)
    l_dot = local(send_dot.at[0], got_dot.at[mine])

    pre = pre_f[...]
    act_f = (pre * sigmoid(pre)).astype(BF16)
    for i in range(2):
        a = dot(act_f, dn[:, pl.ds(i * PART, PART)]).reshape(8, CAP, PART)
        b = dot(act_f, dn[:, pl.ds(HALF + i * PART, PART)]).reshape(8, CAP, PART)
        out_f[i] = jnp.concatenate([a, b], axis=1).astype(BF16)
        push(out_f.at[i, pl.ds(4, 4)], pr_f.at[i], pair, back_f + i)

    hs_b, hr_b, hs_f, hr_f = ids(8), ids(8), ids(8), ids(8)

    def finish(i, out, pr, fs, fin, arrived, s_id, r_id):
        got(pr.at[i], arrived + i)
        for k in (3, 2, 1, 0):
            fs[i, k] = (out[i, k].astype(F32) + pr[i, k].astype(F32)).astype(BF16)
            push(fs.at[i, k], fin.at[i, e], at(shift(-k), pp=nxt), s_id + i * 4 + k, r_id + i * 4 + e)

    for i in range(2):
        finish(i, out_b, pr_b, fs_b, fin_b, back_b, hs_b, hr_b)

    from_sibling(my_w, 16)
    from_sibling(their_w, 17)
    for step in range(4):
        for idx, n in ring_blocks(step):
            from_sibling(idx, n)

    def scores(x):
        total = jnp.zeros((TOK, EXPERTS), F32)
        for i in range(4):
            w = wg[0, pl.ds(4 * i, 4)].reshape(896, EXPERTS)
            total = total + dot(x[:, pl.ds(896 * i, 896)], w)
        return sigmoid(total)

    score_f = scores(xf)
    score_b = scores(xb)
    sum_f = jnp.sum(mask_f * score_f, axis=1, keepdims=True)
    sum_b = jnp.sum(mask_b * score_b, axis=1, keepdims=True)
    gate_f = sel_f * to_slots(ROUTE_SCALE * score_f / sum_f)
    gate_b = sel_b * to_slots(ROUTE_SCALE * score_b / sum_b)
    msg[0], msg[1] = two_parts(gate_f)
    msg[2], msg[3] = two_parts(gate_b)
    mg = ids(1)
    push(msg, msg_in, at(y, pp=nxt), mg)

    l_dot.wait()
    for k in range(1, 8):
        source = (mine + k) % 8
        got(got_dot.at[source], dt_r + source)
    all_dots = got_dot[...].reshape(FLIGHT, 2, CAP, 128)
    slot_dots = (all_dots[:, 0] + all_dots[:, 1]).reshape(SLOTS, 128)
    slot_row = lax.broadcasted_iota(jnp.int32, (SLOTS, EXPERTS), 0)
    slot_col = lax.broadcasted_iota(jnp.int32, (SLOTS, EXPERTS), 1)
    by_expert = jnp.where(
        slot_row // CAP == slot_col, jnp.broadcast_to(slot_dots[:, 0:1], (SLOTS, EXPERTS)), 0.0
    )
    gate_grad = exact(sel_b[:, :SLOTS], by_expert)
    weighted = jnp.sum(gate_grad * score_b, axis=1, keepdims=True) / sum_b
    pick_grad = ROUTE_SCALE / sum_b * (gate_grad - weighted)
    logit_grad = (mask_b * pick_grad * score_b * (1.0 - score_b)).astype(BF16)
    lg[...] = logit_grad
    lid = ids(1)
    push(lg, lg_in, at(y, pp=nxt), lid)

    for i in range(2):
        finish(i, out_f, pr_f, fs_f, fin_f, back_f, hs_f, hr_f)

    def halves(fin, i):
        t = fin[i].astype(F32)
        return t[:, :CAP].reshape(SLOTS, PART).astype(BF16), t[:, CAP:].reshape(SLOTS, PART).astype(BF16)

    def arrived(fin, i, r_id):
        for k in range(4):
            source = (e + k) % 4
            got(fin.at[i, source], r_id + i * 4 + source)

    def router(i):
        return across(lg_in[...], wg[1, pl.ds(4 * i, 4)].reshape(PART, EXPERTS))

    got(msg_in, mg)
    got(lg_in, lid)
    f_high, f_low = msg_in[0][:, :SLOTS], msg_in[1][:, :SLOTS]
    b_high, b_low = msg_in[2][:, :SLOTS], msg_in[3][:, :SLOTS]
    for i in range(2):
        arrived(fin_b, i, hr_b)
        a, b = halves(fin_b, i)
        ob_ref[:, pl.ds(i * PART, PART)] = (dot(b_high, a) + dot(b_low, a) + router(i)).astype(BF16)
        ob_ref[:, pl.ds(HALF + i * PART, PART)] = (dot(b_high, b) + dot(b_low, b) + router(2 + i)).astype(BF16)
    for i in range(2):
        arrived(fin_f, i, hr_f)
        a, b = halves(fin_f, i)
        of_ref[:, pl.ds(i * PART, PART)] = (dot(f_high, a) + dot(f_low, a)).astype(BF16)
        of_ref[:, pl.ds(HALF + i * PART, PART)] = (dot(f_high, b) + dot(f_low, b)).astype(BF16)

    for cp in sends:
        cp.wait_send()


N_SEM = 192


def on_device(xf, xb, g, rf, rb, w, up, dn):
    vm = pltpu.VMEM
    scratch = [
        vm((TOK, D), BF16), vm((TOK, D), BF16), vm((TOK, D), BF16),
        vm((D, 4 * HID), BF16), vm((4 * HID, D), BF16), vm((2, 16, 2, WROWS, EXPERTS), BF16),
        vm((FLIGHT, 16, D), BF16), vm((FLIGHT, 16, HALF), BF16),
        vm((8, 16, D), BF16), vm((8, 16, HALF), BF16),
        vm((64, 4 * HID), F32), vm((64, 4 * HID), F32), vm((64, 4 * HID), F32),
        vm((8, CAP, 128), F32), vm((8, CAP, 128), F32),
        vm((2, 8, 16, PART), BF16), vm((2, 8, 16, PART), BF16),
        vm((2, 4, 16, PART), BF16), vm((2, 4, 16, PART), BF16),
        vm((2, 4, 16, PART), BF16), vm((2, 4, 16, PART), BF16),
        vm((2, 4, 16, PART), BF16), vm((2, 4, 16, PART), BF16),
        vm((4, TOK, 128), BF16), vm((4, TOK, 128), BF16),
        vm((TOK, EXPERTS), BF16), vm((TOK, EXPERTS), BF16),
        pltpu.SemaphoreType.DMA((16,)),
        pltpu.SemaphoreType.DMA((N_SEM,)),
        pltpu.SemaphoreType.DMA((N_SEM,)),
    ]
    hbm = pl.BlockSpec(memory_space=pl.ANY)
    vmem = pl.BlockSpec(memory_space=pltpu.VMEM)
    of, ob = pl.pallas_call(
        kernel,
        out_shape=[jax.ShapeDtypeStruct((TOK, D), BF16)] * 2,
        in_specs=[hbm, hbm, hbm, vmem, vmem, hbm, hbm, hbm],
        out_specs=[vmem, vmem],
        scratch_shapes=scratch,
        compiler_params=pltpu.CompilerParams(
            collective_id=0, has_side_effects=True, vmem_limit_bytes=60 * 2**20
        ),
        cost_estimate=pl.CostEstimate(flops=2 * 10**9, bytes_accessed=6 * 10**6, transcendentals=10**5),
        name="expert_layer",
    )(xf[0], xb[0], g[0], rf[0].T, rb[0].T, w[0], up[0], dn[0])
    return of[None], ob[None]


def solution(mesh):
    rows = P("pipe", "expert", None)
    return jax.shard_map(
        on_device,
        mesh=mesh,
        in_specs=(rows, rows, rows, rows, rows, rows, P("pipe", None, "expert"), rows),
        out_specs=(rows, rows),
        check_vma=False,
    )
```

```python
import functools

import jax
import jax.numpy as jnp
from jax import lax
from jax.experimental import pallas as pl
from jax.experimental.pallas import tpu as pltpu
from jax.sharding import PartitionSpec as P

MESH = pl.DeviceIdType.MESH
D = 3584
HALF = D // 2
PART = HALF // 2
EXPERTS = 256
CAP = 8
FLIGHT = 4
SLOTS = FLIGHT * CAP
TOK = 64
HID = 128
WROWS = 112
NY = 8
DN = 4
SECTIONS = 16
ROUTE_SCALE = 2.5
HIGHEST = lax.Precision.HIGHEST
F32 = jnp.float32
BF16 = jnp.bfloat16
OFFSETS = (-1, 2, -3)


def across(a, b):
    return lax.dot_general(a, b, (((1,), (1,)), ((), ())), preferred_element_type=F32)


def dot(a, b):
    return jnp.dot(a, b, preferred_element_type=F32)


def exact(a, b):
    return jnp.dot(a, b, preferred_element_type=F32, precision=HIGHEST)


def sigmoid(v):
    return 1.0 / (1.0 + jnp.exp(-v))


def chosen_mask(routes_ref):
    wide = jnp.concatenate([routes_ref[...].astype(F32)] * 2, axis=1)
    routes = wide.T[:TOK]
    ids = lax.broadcasted_iota(jnp.int32, (TOK, EXPERTS), 1).astype(F32)
    mask = jnp.zeros((TOK, EXPERTS), F32)
    for k in range(routes_ref.shape[0]):
        mask = mask + jnp.where(routes[:, k : k + 1] == ids, 1.0, 0.0)
    return mask


def two_parts(v):
    high = v.astype(BF16)
    return high, (v - high.astype(F32)).astype(BF16)


def to_slots(columns):
    lane = lax.broadcasted_iota(jnp.int32, (TOK, 128), 1)
    out = jnp.zeros((TOK, 128), F32)
    for e in range(FLIGHT):
        inside = (lane >= e * CAP) & (lane < (e + 1) * CAP)
        out = out + jnp.where(inside, jnp.broadcast_to(columns[:, e : e + 1], (TOK, 128)), 0.0)
    return out


def slot_select(mask):
    member = to_slots(mask)
    row = lax.broadcasted_iota(jnp.int32, (TOK, TOK), 0)
    col = lax.broadcasted_iota(jnp.int32, (TOK, TOK), 1)
    below = jnp.where(col < row, 1.0, 0.0).astype(BF16)
    placing = dot(below, member.astype(BF16))
    lane = lax.broadcasted_iota(jnp.int32, (TOK, 128), 1)
    slot = (lane % CAP).astype(F32)
    return jnp.where(placing == slot, member, 0.0)


def kernel(
    xf_hbm, xb_hbm, g_hbm, rf_ref, rb_ref, w_hbm, up_hbm, dn_hbm,
    of_ref, ob_ref,
    xf, xb, g, up, dn, wg, pb, pf, rows_b, rows_f,
    pre_b, grad_b, pre_f, send_dot, got_dot, out_b, out_f,
    pr_b, pr_f, fs_b, fs_f, fin_b, fin_f,
    msg, msg_in, lg, lg_in,
    lsem, ssem, rsem,
):
    p = lax.axis_index("pipe")
    me = lax.axis_index("expert")
    y = me // 4
    xh = (me // 2) % 2
    c = me % 2
    e = y // 2
    sig = 1 - 2 * (y % 2)
    nxt = (p + 1) % SECTIONS
    prv = (p + SECTIONS - 1) % SECTIONS

    def at(yy, xx=None, cc=None, pp=None):
        xx = xh if xx is None else xx
        cc = c if cc is None else cc
        return (p if pp is None else pp, (yy * 2 + xx) * 2 + cc)

    def shift(off):
        return (y + NY + sig * off) % NY

    def slot_y(s):
        return shift(-s) if s < 4 else shift(s - 3)

    sib = at(y, cc=1 - c)
    xpart = at(y, xx=1 - xh)
    pair = at(shift(1))

    bar = pltpu.get_barrier_semaphore()

    def greet(dev):
        pl.semaphore_signal(bar, inc=1, device_id=dev, device_id_type=MESH)

    for s in range(1, 8):
        greet(at(slot_y(s)))
    greet(xpart)
    greet(sib)
    greet(at(y, pp=prv))
    greet(at(y, xx=1 - xh, pp=prv))
    for off in OFFSETS:
        greet(at(shift(off), pp=prv))

    nsem = [0]
    nlocal = [0]
    sends = []

    def ids(n):
        first = nsem[0]
        nsem[0] += n
        return first

    def local(src, dst):
        cp = pltpu.make_async_copy(src, dst, lsem.at[nlocal[0]])
        nlocal[0] += 1
        cp.start()
        return cp

    def push(src, dst, dev, s_id, r_id=None):
        cp = pltpu.make_async_remote_copy(
            src_ref=src, dst_ref=dst, send_sem=ssem.at[s_id],
            recv_sem=rsem.at[s_id if r_id is None else r_id],
            device_id=dev, device_id_type=MESH,
        )
        cp.start()
        sends.append(cp)

    def got(dst, r_id):
        pltpu.make_async_remote_copy(
            src_ref=dst, dst_ref=dst, send_sem=ssem.at[0], recv_sem=rsem.at[r_id],
            device_id=sib, device_id_type=MESH,
        ).wait_recv()

    l_xb = local(xb_hbm, xb)
    l_g = local(g_hbm, g)
    l_xf = local(xf_hbm, xf)
    l_up = local(up_hbm, up.at[:, pl.ds(0, HID)])
    l_dn = local(dn_hbm, dn.at[pl.ds(0, HID)])
    my_w = y * 2 + xh
    l_w = local(w_hbm, wg.at[0, my_w, c])

    mask_b = chosen_mask(rb_ref)
    mask_f = chosen_mask(rf_ref)
    sel_b = slot_select(mask_b)
    sel_f = slot_select(mask_f)
    pick_b = sel_b.T[:SLOTS].astype(BF16)
    pick_f = sel_f.T[:SLOTS].astype(BF16)

    l_xb.wait()
    l_g.wait()
    for i in range(7):
        cols = pl.ds(i * 512, 512)
        a = dot(pick_b, xb[:, cols]).reshape(FLIGHT, CAP, 512)
        b = dot(pick_b, g[:, cols]).reshape(FLIGHT, CAP, 512)
        pb[:, :, cols] = jnp.concatenate([a, b], axis=1).astype(BF16)

    pl.semaphore_wait(bar, 14)

    def up_part(k, rows):
        return up.at[rows, pl.ds(k * HID, HID)]

    def dn_part(k, rows):
        return dn.at[pl.ds(k * HID + rows.start, rows.size)]

    up_rows = [pl.ds(i * HALF, HALF) for i in range(2)]
    dn_rows = [pl.ds(i * (HID // DN), HID // DN) for i in range(DN)]
    ux, us, uy, dx, ds_, dy = ids(2), ids(2), ids(2), ids(DN), ids(DN), ids(DN)

    def enter(src, rows, iy):
        push(src.at[e], rows.at[4], pair, iy + 4)
        for off in OFFSETS:
            t = shift(off)
            push(src.at[t // 2], rows.at[abs(off)], at(t), iy + abs(off))
        return local(src.at[e], rows.at[0])

    def hands(rows, iy, slots):
        for s in slots:
            got(rows.at[s], iy + s)
            push(rows.at[s], rows.at[4 + s], pair, iy + 4 + s)

    iy_b, iy_f = ids(8), ids(8)
    l_b0 = enter(pb, rows_b, iy_b)
    for i in range(2):
        push(up_hbm.at[up_rows[i]], up_part(1, up_rows[i]), sib, us + i)
    for i in range(DN):
        push(dn_hbm.at[dn_rows[i]], dn_part(1, dn_rows[i]), sib, ds_ + i)
    wx = ids(3)
    push(w_hbm, wg.at[0, my_w, c], xpart, wx)
    push(w_hbm, wg.at[1, my_w, c], at(y, pp=nxt), wx + 1)
    push(w_hbm, wg.at[1, my_w, c], at(y, xx=1 - xh, pp=nxt), wx + 2)

    l_xf.wait()
    for i in range(7):
        lo = pl.ds(i * 256, 256)
        hi = pl.ds(HALF + i * 256, 256)
        a = dot(pick_f, xf[:, lo]).reshape(FLIGHT, CAP, 256)
        b = dot(pick_f, xf[:, hi]).reshape(FLIGHT, CAP, 256)
        pf[:, :, lo] = jnp.concatenate([a, b], axis=1).astype(BF16)

    l_f0 = enter(pf, rows_f, iy_f)

    up_dev, down_dev = at((y + 1) % NY), at((y + NY - 1) % NY)
    wr = ids(16)

    def ring(step):
        yu = (y + NY - step) % NY
        yd = (y + step) % NY
        for xx in range(2):
            if step < 3 or xx == 0:
                push(wg.at[:, yu * 2 + xx, c], wg.at[:, yu * 2 + xx, c], up_dev, wr + step * 2 + xx)
            if step < 3 or xx == 1:
                push(wg.at[:, yd * 2 + xx, c], wg.at[:, yd * 2 + xx, c], down_dev, wr + 8 + step * 2 + xx)

    wsib = ids(18)

    def to_sibling(idx, n):
        push(wg.at[:, idx, c], wg.at[:, idx, c], sib, wsib + n)

    def from_sibling(idx, n):
        got(wg.at[:, idx, 1 - c], wsib + n)

    def ring_blocks(step):
        yu = (y + NY - step - 1) % NY
        yd = (y + step + 1) % NY
        for xx in range(2):
            if step < 3 or xx == 0:
                yield yu * 2 + xx, step * 2 + xx
            if step < 3 or xx == 1:
                yield yd * 2 + xx, 8 + step * 2 + xx

    def ring_got(step):
        for idx, n in ring_blocks(step):
            got(wg.at[:, idx, c], wr + n)
            to_sibling(idx, n)

    own, other = pl.ds(0, 2 * HID), pl.ds(2 * HID, 2 * HID)

    def forward_pre(lanes):
        r = rows_f[...].reshape(128, HALF)
        low = dot(r, up[pl.ds(0, HALF), lanes]).reshape(8, 16, 256)[:, :CAP]
        high = dot(r, up[pl.ds(HALF, HALF), lanes]).reshape(8, 16, 256)[:, CAP:]
        pre_f[:, lanes] = (low + high).reshape(64, 256)

    def backward_pre(lanes):
        r = rows_b[...].reshape(128, D)
        pre_b[:, lanes] = dot(r, up[:, lanes]).reshape(8, 16, 256)[:, :CAP].reshape(64, 256)

    def backward_grad(lanes):
        r = rows_b[...].reshape(128, D)
        grad_b[:, lanes] = across(r, dn[lanes, :]).reshape(8, 16, 256)[:, CAP:].reshape(64, 256)


    def up_on(i):
        got(up_part(2, up_rows[i]), ux + i)
        push(up_part(2, up_rows[i]), up_part(3, up_rows[i]), sib, uy + i)

    def dn_on(i):
        got(dn_part(2, dn_rows[i]), dx + i)
        push(dn_part(2, dn_rows[i]), dn_part(3, dn_rows[i]), sib, dy + i)

    def send_up(i):
        push(up_hbm.at[up_rows[i]], up_part(2, up_rows[i]), xpart, ux + i)

    def send_dn(i):
        push(dn_hbm.at[dn_rows[i]], dn_part(2, dn_rows[i]), xpart, dx + i)

    send_up(0)
    send_up(1)
    for i in range(DN):
        send_dn(i)
    hands(rows_b, iy_b, (1,))
    l_w.wait()
    their_w = y * 2 + (1 - xh)
    got(wg.at[0, their_w, c], wx)
    got(wg.at[1, my_w, c], wx + 1)
    got(wg.at[1, their_w, c], wx + 2)
    ring(0)
    to_sibling(my_w, 16)
    to_sibling(their_w, 17)
    hands(rows_b, iy_b, (2, 3))
    hands(rows_f, iy_f, (1, 2, 3))
    ring_got(0)
    ring(1)
    l_b0.wait()
    l_f0.wait()
    l_up.wait()
    l_dn.wait()
    for i in range(2):
        got(up_part(1, up_rows[i]), us + i)
    for i in range(DN):
        got(dn_part(1, dn_rows[i]), ds_ + i)
    for s in range(4, 8):
        got(rows_b.at[s], iy_b + s)
    backward_pre(own)
    backward_grad(own)
    ring_got(1)
    ring(2)
    up_on(0)
    for s in range(4, 8):
        got(rows_f.at[s], iy_f + s)
    forward_pre(own)
    ring_got(2)
    ring(3)
    up_on(1)
    for i in range(2):
        got(up_part(3, up_rows[i]), uy + i)
    backward_pre(other)
    forward_pre(other)
    ring_got(3)
    for i in range(DN):
        dn_on(i)
    for i in range(DN):
        got(dn_part(3, dn_rows[i]), dy + i)
    back_b, back_f = ids(2), ids(2)
    pre = pre_f[...]
    act_f = (pre * sigmoid(pre)).astype(BF16)
    for i in range(2):
        a = dot(act_f, dn[:, pl.ds(i * PART, PART)]).reshape(8, CAP, PART)
        b = dot(act_f, dn[:, pl.ds(HALF + i * PART, PART)]).reshape(8, CAP, PART)
        out_f[i] = jnp.concatenate([a, b], axis=1).astype(BF16)
        push(out_f.at[i, pl.ds(4, 4)], pr_f.at[i], pair, back_f + i)

    backward_grad(other)
    pre = pre_b[...]
    act_grad = grad_b[...]
    s = sigmoid(pre)
    act = (pre * s).astype(BF16).astype(F32)
    dots = jnp.sum(act * act_grad, axis=1, keepdims=True)
    send_dot[...] = jnp.broadcast_to(dots, (64, 128)).reshape(8, CAP, 128)
    pre_grad = (act_grad * (s * (1.0 + pre * (1.0 - s)))).astype(BF16)
    for i in range(2):
        a = across(pre_grad, up[pl.ds(i * PART, PART), :]).reshape(8, CAP, PART)
        b = across(pre_grad, up[pl.ds(HALF + i * PART, PART), :]).reshape(8, CAP, PART)
        out_b[i] = jnp.concatenate([a, b], axis=1).astype(BF16)
        push(out_b.at[i, pl.ds(4, 4)], pr_b.at[i], pair, back_b + i)
    mine = e * 2 + y % 2
    dt_s, dt_r = ids(8), ids(8)
    for k in range(1, 8):
        push(send_dot.at[k], got_dot.at[mine], at(slot_y(k)), dt_s + k, dt_r + mine)
    l_dot = local(send_dot.at[0], got_dot.at[mine])

    hs_b, hr_b, hs_f, hr_f = ids(8), ids(8), ids(8), ids(8)

    def finish(i, out, pr, fs, fin, arrived, s_id, r_id):
        got(pr.at[i], arrived + i)
        for k in (3, 2, 1, 0):
            fs[i, k] = (out[i, k].astype(F32) + pr[i, k].astype(F32)).astype(BF16)
            push(fs.at[i, k], fin.at[i, e], at(shift(-k), pp=nxt), s_id + i * 4 + k, r_id + i * 4 + e)

    for i in range(2):
        finish(i, out_f, pr_f, fs_f, fin_f, back_f, hs_f, hr_f)

    from_sibling(my_w, 16)
    from_sibling(their_w, 17)
    for step in range(4):
        for idx, n in ring_blocks(step):
            from_sibling(idx, n)

    def scores(x):
        total = jnp.zeros((TOK, EXPERTS), F32)
        for i in range(4):
            w = wg[0, pl.ds(4 * i, 4)].reshape(896, EXPERTS)
            total = total + dot(x[:, pl.ds(896 * i, 896)], w)
        return sigmoid(total)

    score_f = scores(xf)
    score_b = scores(xb)
    sum_f = jnp.sum(mask_f * score_f, axis=1, keepdims=True)
    sum_b = jnp.sum(mask_b * score_b, axis=1, keepdims=True)
    gate_f = sel_f * to_slots(ROUTE_SCALE * score_f / sum_f)
    gate_b = sel_b * to_slots(ROUTE_SCALE * score_b / sum_b)
    msg[0], msg[1] = two_parts(gate_f)
    msg[2], msg[3] = two_parts(gate_b)
    mg = ids(1)
    push(msg, msg_in, at(y, pp=nxt), mg)

    for i in range(2):
        finish(i, out_b, pr_b, fs_b, fin_b, back_b, hs_b, hr_b)

    l_dot.wait()
    for k in range(1, 8):
        source = (mine + k) % 8
        got(got_dot.at[source], dt_r + source)
    all_dots = got_dot[...].reshape(FLIGHT, 2, CAP, 128)
    slot_dots = (all_dots[:, 0] + all_dots[:, 1]).reshape(SLOTS, 128)
    slot_row = lax.broadcasted_iota(jnp.int32, (SLOTS, EXPERTS), 0)
    slot_col = lax.broadcasted_iota(jnp.int32, (SLOTS, EXPERTS), 1)
    by_expert = jnp.where(
        slot_row // CAP == slot_col, jnp.broadcast_to(slot_dots[:, 0:1], (SLOTS, EXPERTS)), 0.0
    )
    gate_grad = exact(sel_b[:, :SLOTS], by_expert)
    weighted = jnp.sum(gate_grad * score_b, axis=1, keepdims=True) / sum_b
    pick_grad = ROUTE_SCALE / sum_b * (gate_grad - weighted)
    logit_grad = (mask_b * pick_grad * score_b * (1.0 - score_b)).astype(BF16)
    lg[...] = logit_grad
    lid = ids(1)
    push(lg, lg_in, at(y, pp=nxt), lid)

    def halves(fin, i):
        t = fin[i].astype(F32)
        return t[:, :CAP].reshape(SLOTS, PART).astype(BF16), t[:, CAP:].reshape(SLOTS, PART).astype(BF16)

    def arrived(fin, i, r_id):
        for k in range(4):
            source = (e + k) % 4
            got(fin.at[i, source], r_id + i * 4 + source)

    def router(i):
        return across(lg_in[...], wg[1, pl.ds(4 * i, 4)].reshape(PART, EXPERTS))

    got(msg_in, mg)
    f_high, f_low = msg_in[0][:, :SLOTS], msg_in[1][:, :SLOTS]
    b_high, b_low = msg_in[2][:, :SLOTS], msg_in[3][:, :SLOTS]
    for i in range(2):
        arrived(fin_f, i, hr_f)
        a, b = halves(fin_f, i)
        of_ref[:, pl.ds(i * PART, PART)] = (dot(f_high, a) + dot(f_low, a)).astype(BF16)
        of_ref[:, pl.ds(HALF + i * PART, PART)] = (dot(f_high, b) + dot(f_low, b)).astype(BF16)
    got(lg_in, lid)
    for i in range(2):
        arrived(fin_b, i, hr_b)
        a, b = halves(fin_b, i)
        ob_ref[:, pl.ds(i * PART, PART)] = (dot(b_high, a) + dot(b_low, a) + router(i)).astype(BF16)
        ob_ref[:, pl.ds(HALF + i * PART, PART)] = (dot(b_high, b) + dot(b_low, b) + router(2 + i)).astype(BF16)

    for cp in sends:
        cp.wait_send()


N_SEM = 192


def on_device(xf, xb, g, rf, rb, w, up, dn):
    vm = pltpu.VMEM
    scratch = [
        vm((TOK, D), BF16), vm((TOK, D), BF16), vm((TOK, D), BF16),
        vm((D, 4 * HID), BF16), vm((4 * HID, D), BF16), vm((2, 16, 2, WROWS, EXPERTS), BF16),
        vm((FLIGHT, 16, D), BF16), vm((FLIGHT, 16, HALF), BF16),
        vm((8, 16, D), BF16), vm((8, 16, HALF), BF16),
        vm((64, 4 * HID), F32), vm((64, 4 * HID), F32), vm((64, 4 * HID), F32),
        vm((8, CAP, 128), F32), vm((8, CAP, 128), F32),
        vm((2, 8, 16, PART), BF16), vm((2, 8, 16, PART), BF16),
        vm((2, 4, 16, PART), BF16), vm((2, 4, 16, PART), BF16),
        vm((2, 4, 16, PART), BF16), vm((2, 4, 16, PART), BF16),
        vm((2, 4, 16, PART), BF16), vm((2, 4, 16, PART), BF16),
        vm((4, TOK, 128), BF16), vm((4, TOK, 128), BF16),
        vm((TOK, EXPERTS), BF16), vm((TOK, EXPERTS), BF16),
        pltpu.SemaphoreType.DMA((16,)),
        pltpu.SemaphoreType.DMA((N_SEM,)),
        pltpu.SemaphoreType.DMA((N_SEM,)),
    ]
    hbm = pl.BlockSpec(memory_space=pl.ANY)
    vmem = pl.BlockSpec(memory_space=pltpu.VMEM)
    of, ob = pl.pallas_call(
        kernel,
        out_shape=[pltpu.VMEM((TOK, D), BF16)] * 2,
        in_specs=[hbm, hbm, hbm, vmem, vmem, hbm, hbm, hbm],
        out_specs=[vmem, vmem],
        scratch_shapes=scratch,
        compiler_params=pltpu.CompilerParams(
            collective_id=0, has_side_effects=True, vmem_limit_bytes=60 * 2**20
        ),
        cost_estimate=pl.CostEstimate(flops=2 * 10**9, bytes_accessed=6 * 10**6, transcendentals=10**5),
        name="expert_layer",
    )(xf[0], xb[0], g[0], rf[0].T, rb[0].T, w[0], up[0], dn[0])
    return of[None], ob[None]


def solution(mesh):
    rows = P("pipe", "expert", None)
    return jax.shard_map(
        on_device,
        mesh=mesh,
        in_specs=(rows, rows, rows, rows, rows, rows, P("pipe", None, "expert"), rows),
        out_specs=(rows, rows),
        check_vma=False,
    )
```

```python
import functools

import jax
import jax.numpy as jnp
from jax import lax
from jax.experimental import pallas as pl
from jax.experimental.pallas import tpu as pltpu
from jax.sharding import PartitionSpec as P

MESH = pl.DeviceIdType.MESH
D = 3584
HALF = D // 2
PART = HALF // 2
EXPERTS = 256
CAP = 8
FLIGHT = 4
SLOTS = FLIGHT * CAP
TOK = 64
HID = 128
WROWS = 112
NY = 8
DN = 4
SECTIONS = 16
ROUTE_SCALE = 2.5
HIGHEST = lax.Precision.HIGHEST
F32 = jnp.float32
BF16 = jnp.bfloat16
OFFSETS = (-1, 2, -3)


def across(a, b):
    return lax.dot_general(a, b, (((1,), (1,)), ((), ())), preferred_element_type=F32)


def dot(a, b):
    return jnp.dot(a, b, preferred_element_type=F32)


def exact(a, b):
    return jnp.dot(a, b, preferred_element_type=F32, precision=HIGHEST)


def sigmoid(v):
    return 1.0 / (1.0 + jnp.exp(-v))


def chosen_mask(routes_ref):
    wide = jnp.concatenate([routes_ref[...].astype(F32)] * 2, axis=1)
    routes = wide.T[:TOK]
    ids = lax.broadcasted_iota(jnp.int32, (TOK, EXPERTS), 1).astype(F32)
    mask = jnp.zeros((TOK, EXPERTS), F32)
    for k in range(routes_ref.shape[0]):
        mask = mask + jnp.where(routes[:, k : k + 1] == ids, 1.0, 0.0)
    return mask


def two_parts(v):
    high = v.astype(BF16)
    return high, (v - high.astype(F32)).astype(BF16)


def to_slots(columns):
    lane = lax.broadcasted_iota(jnp.int32, (TOK, 128), 1)
    out = jnp.zeros((TOK, 128), F32)
    for e in range(FLIGHT):
        inside = (lane >= e * CAP) & (lane < (e + 1) * CAP)
        out = out + jnp.where(inside, jnp.broadcast_to(columns[:, e : e + 1], (TOK, 128)), 0.0)
    return out


def slot_select(mask):
    member = to_slots(mask)
    row = lax.broadcasted_iota(jnp.int32, (TOK, TOK), 0)
    col = lax.broadcasted_iota(jnp.int32, (TOK, TOK), 1)
    below = jnp.where(col < row, 1.0, 0.0).astype(BF16)
    placing = dot(below, member.astype(BF16))
    lane = lax.broadcasted_iota(jnp.int32, (TOK, 128), 1)
    slot = (lane % CAP).astype(F32)
    return jnp.where(placing == slot, member, 0.0)


def kernel(
    xf_hbm, xb_hbm, g_hbm, rf_ref, rb_ref, w_hbm, up_hbm, dn_hbm,
    of_ref, ob_ref,
    xf, xb, g, up, dn, wg, pb, pf, rows_b, rows_f,
    pre_b, grad_b, pre_f, send_dot, got_dot, out_b, out_f,
    pr_b, pr_f, fs_b, fs_f, fin_b, fin_f,
    msg, msg_in, lg, lg_in,
    lsem, ssem, rsem,
):
    p = lax.axis_index("pipe")
    me = lax.axis_index("expert")
    y = me // 4
    xh = (me // 2) % 2
    c = me % 2
    e = y // 2
    sig = 1 - 2 * (y % 2)
    nxt = (p + 1) % SECTIONS
    prv = (p + SECTIONS - 1) % SECTIONS

    def at(yy, xx=None, cc=None, pp=None):
        xx = xh if xx is None else xx
        cc = c if cc is None else cc
        return (p if pp is None else pp, (yy * 2 + xx) * 2 + cc)

    def shift(off):
        return (y + NY + sig * off) % NY

    def slot_y(s):
        return shift(-s) if s < 4 else shift(s - 3)

    sib = at(y, cc=1 - c)
    xpart = at(y, xx=1 - xh)
    pair = at(shift(1))

    bar = pltpu.get_barrier_semaphore()

    def greet(dev):
        pl.semaphore_signal(bar, inc=1, device_id=dev, device_id_type=MESH)

    for s in range(1, 8):
        greet(at(slot_y(s)))
    greet(xpart)
    greet(sib)
    greet(at(y, pp=prv))
    greet(at(y, xx=1 - xh, pp=prv))
    for off in OFFSETS:
        greet(at(shift(off), pp=prv))

    nsem = [0]
    nlocal = [0]
    sends = []

    def ids(n):
        first = nsem[0]
        nsem[0] += n
        return first

    def local(src, dst):
        cp = pltpu.make_async_copy(src, dst, lsem.at[nlocal[0]])
        nlocal[0] += 1
        cp.start()
        return cp

    def push(src, dst, dev, s_id, r_id=None):
        cp = pltpu.make_async_remote_copy(
            src_ref=src, dst_ref=dst, send_sem=ssem.at[s_id],
            recv_sem=rsem.at[s_id if r_id is None else r_id],
            device_id=dev, device_id_type=MESH,
        )
        cp.start()
        sends.append(cp)

    def got(dst, r_id):
        pltpu.make_async_remote_copy(
            src_ref=dst, dst_ref=dst, send_sem=ssem.at[0], recv_sem=rsem.at[r_id],
            device_id=sib, device_id_type=MESH,
        ).wait_recv()

    l_xb = local(xb_hbm, xb)
    l_g = local(g_hbm, g)
    l_xf = local(xf_hbm, xf)
    l_up = local(up_hbm, up.at[:, pl.ds(0, HID)])
    l_dn = local(dn_hbm, dn.at[pl.ds(0, HID)])
    my_w = y * 2 + xh
    l_w = local(w_hbm, wg.at[0, my_w, c])

    mask_b = chosen_mask(rb_ref)
    mask_f = chosen_mask(rf_ref)
    sel_b = slot_select(mask_b)
    sel_f = slot_select(mask_f)
    pick_b = sel_b.T[:SLOTS].astype(BF16)
    pick_f = sel_f.T[:SLOTS].astype(BF16)

    l_xb.wait()
    l_g.wait()
    for i in range(7):
        cols = pl.ds(i * 512, 512)
        a = dot(pick_b, xb[:, cols]).reshape(FLIGHT, CAP, 512)
        b = dot(pick_b, g[:, cols]).reshape(FLIGHT, CAP, 512)
        pb[:, :, cols] = jnp.concatenate([a, b], axis=1).astype(BF16)

    pl.semaphore_wait(bar, 14)

    def up_part(k, rows):
        return up.at[rows, pl.ds(k * HID, HID)]

    def dn_part(k, cols):
        return dn.at[pl.ds(k * HID, HID), cols]

    up_rows = [pl.ds(i * HALF, HALF) for i in range(2)]
    dn_cols = [pl.ds(i * PART, PART) for i in (0, 2, 1, 3)]
    ux, us, uy, dx, ds_, dy = ids(2), ids(2), ids(2), ids(DN), ids(DN), ids(DN)

    def enter(src, rows, iy):
        push(src.at[e], rows.at[4], pair, iy + 4)
        for off in OFFSETS:
            t = shift(off)
            push(src.at[t // 2], rows.at[abs(off)], at(t), iy + abs(off))
        return local(src.at[e], rows.at[0])

    def hands(rows, iy, slots):
        for s in slots:
            got(rows.at[s], iy + s)
            push(rows.at[s], rows.at[4 + s], pair, iy + 4 + s)

    iy_b, iy_f = ids(8), ids(8)
    l_b0 = enter(pb, rows_b, iy_b)
    for i in range(2):
        push(up_hbm.at[up_rows[i]], up_part(1, up_rows[i]), sib, us + i)
    for i in range(DN):
        push(dn_hbm.at[:, dn_cols[i]], dn_part(1, dn_cols[i]), sib, ds_ + i)
    wx = ids(3)
    push(w_hbm, wg.at[0, my_w, c], xpart, wx)
    push(w_hbm, wg.at[1, my_w, c], at(y, pp=nxt), wx + 1)
    push(w_hbm, wg.at[1, my_w, c], at(y, xx=1 - xh, pp=nxt), wx + 2)

    l_xf.wait()
    for i in range(7):
        lo = pl.ds(i * 256, 256)
        hi = pl.ds(HALF + i * 256, 256)
        a = dot(pick_f, xf[:, lo]).reshape(FLIGHT, CAP, 256)
        b = dot(pick_f, xf[:, hi]).reshape(FLIGHT, CAP, 256)
        pf[:, :, lo] = jnp.concatenate([a, b], axis=1).astype(BF16)

    l_f0 = enter(pf, rows_f, iy_f)

    up_dev, down_dev = at((y + 1) % NY), at((y + NY - 1) % NY)
    wr = ids(16)

    def ring(step):
        yu = (y + NY - step) % NY
        yd = (y + step) % NY
        for xx in range(2):
            if step < 3 or xx == 0:
                push(wg.at[:, yu * 2 + xx, c], wg.at[:, yu * 2 + xx, c], up_dev, wr + step * 2 + xx)
            if step < 3 or xx == 1:
                push(wg.at[:, yd * 2 + xx, c], wg.at[:, yd * 2 + xx, c], down_dev, wr + 8 + step * 2 + xx)

    wsib = ids(18)

    def to_sibling(idx, n):
        push(wg.at[:, idx, c], wg.at[:, idx, c], sib, wsib + n)

    def from_sibling(idx, n):
        got(wg.at[:, idx, 1 - c], wsib + n)

    def ring_blocks(step):
        yu = (y + NY - step - 1) % NY
        yd = (y + step + 1) % NY
        for xx in range(2):
            if step < 3 or xx == 0:
                yield yu * 2 + xx, step * 2 + xx
            if step < 3 or xx == 1:
                yield yd * 2 + xx, 8 + step * 2 + xx

    def ring_got(step):
        for idx, n in ring_blocks(step):
            got(wg.at[:, idx, c], wr + n)
            to_sibling(idx, n)

    own, other = pl.ds(0, 2 * HID), pl.ds(2 * HID, 2 * HID)

    def forward_pre(lanes):
        r = rows_f[...].reshape(128, HALF)
        low = dot(r, up[pl.ds(0, HALF), lanes]).reshape(8, 16, 256)[:, :CAP]
        high = dot(r, up[pl.ds(HALF, HALF), lanes]).reshape(8, 16, 256)[:, CAP:]
        pre_f[:, lanes] = (low + high).reshape(64, 256)

    def backward_pre(lanes):
        r = rows_b[...].reshape(128, D)
        pre_b[:, lanes] = dot(r, up[:, lanes]).reshape(8, 16, 256)[:, :CAP].reshape(64, 256)

    def backward_grad(lanes):
        r = rows_b[...].reshape(128, D)
        grad_b[:, lanes] = across(r, dn[lanes, :]).reshape(8, 16, 256)[:, CAP:].reshape(64, 256)


    def up_on(i):
        got(up_part(2, up_rows[i]), ux + i)
        push(up_part(2, up_rows[i]), up_part(3, up_rows[i]), sib, uy + i)

    def dn_on(i):
        got(dn_part(2, dn_cols[i]), dx + i)
        push(dn_part(2, dn_cols[i]), dn_part(3, dn_cols[i]), sib, dy + i)

    def send_up(i):
        push(up_hbm.at[up_rows[i]], up_part(2, up_rows[i]), xpart, ux + i)

    def send_dn(i):
        push(dn_hbm.at[:, dn_cols[i]], dn_part(2, dn_cols[i]), xpart, dx + i)

    send_up(0)
    send_up(1)
    for i in range(DN):
        send_dn(i)
    hands(rows_b, iy_b, (1,))
    l_w.wait()
    their_w = y * 2 + (1 - xh)
    got(wg.at[0, their_w, c], wx)
    got(wg.at[1, my_w, c], wx + 1)
    got(wg.at[1, their_w, c], wx + 2)
    ring(0)
    to_sibling(my_w, 16)
    to_sibling(their_w, 17)
    hands(rows_b, iy_b, (2, 3))
    hands(rows_f, iy_f, (1, 2, 3))
    ring_got(0)
    ring(1)
    l_b0.wait()
    l_f0.wait()
    l_up.wait()
    l_dn.wait()
    for i in range(2):
        got(up_part(1, up_rows[i]), us + i)
    for i in range(DN):
        got(dn_part(1, dn_cols[i]), ds_ + i)
    for s in range(4, 8):
        got(rows_b.at[s], iy_b + s)
    backward_pre(own)
    backward_grad(own)
    ring_got(1)
    ring(2)
    up_on(0)
    for s in range(4, 8):
        got(rows_f.at[s], iy_f + s)
    forward_pre(own)
    ring_got(2)
    ring(3)
    up_on(1)
    for i in range(2):
        got(up_part(3, up_rows[i]), uy + i)
    backward_pre(other)
    forward_pre(other)
    back_b, back_f = ids(2), ids(2)
    pre = pre_f[...]
    act_f = (pre * sigmoid(pre)).astype(BF16)

    def forward_out(i):
        for j in (2 * i, 2 * i + 1):
            dn_on(j)
        for j in (2 * i, 2 * i + 1):
            got(dn_part(3, dn_cols[j]), dy + j)
        a = dot(act_f, dn[:, pl.ds(i * PART, PART)]).reshape(8, CAP, PART)
        b = dot(act_f, dn[:, pl.ds(HALF + i * PART, PART)]).reshape(8, CAP, PART)
        out_f[i] = jnp.concatenate([a, b], axis=1).astype(BF16)
        push(out_f.at[i, pl.ds(4, 4)], pr_f.at[i], pair, back_f + i)

    forward_out(0)
    ring_got(3)
    forward_out(1)
    backward_grad(other)
    pre = pre_b[...]
    act_grad = grad_b[...]
    s = sigmoid(pre)
    act = (pre * s).astype(BF16).astype(F32)
    dots = jnp.sum(act * act_grad, axis=1, keepdims=True)
    send_dot[...] = jnp.broadcast_to(dots, (64, 128)).reshape(8, CAP, 128)
    pre_grad = (act_grad * (s * (1.0 + pre * (1.0 - s)))).astype(BF16)
    for i in range(2):
        a = across(pre_grad, up[pl.ds(i * PART, PART), :]).reshape(8, CAP, PART)
        b = across(pre_grad, up[pl.ds(HALF + i * PART, PART), :]).reshape(8, CAP, PART)
        out_b[i] = jnp.concatenate([a, b], axis=1).astype(BF16)
        push(out_b.at[i, pl.ds(4, 4)], pr_b.at[i], pair, back_b + i)
    mine = e * 2 + y % 2
    dt_s, dt_r = ids(8), ids(8)
    for k in range(1, 8):
        push(send_dot.at[k], got_dot.at[mine], at(slot_y(k)), dt_s + k, dt_r + mine)
    l_dot = local(send_dot.at[0], got_dot.at[mine])

    hs_b, hr_b, hs_f, hr_f = ids(8), ids(8), ids(8), ids(8)

    def finish(i, out, pr, fs, fin, arrived, s_id, r_id):
        got(pr.at[i], arrived + i)
        for k in (3, 2, 1, 0):
            fs[i, k] = (out[i, k].astype(F32) + pr[i, k].astype(F32)).astype(BF16)
            push(fs.at[i, k], fin.at[i, e], at(shift(-k), pp=nxt), s_id + i * 4 + k, r_id + i * 4 + e)

    for i in range(2):
        finish(i, out_f, pr_f, fs_f, fin_f, back_f, hs_f, hr_f)

    from_sibling(my_w, 16)
    from_sibling(their_w, 17)
    for step in range(4):
        for idx, n in ring_blocks(step):
            from_sibling(idx, n)

    def scores(x):
        total = jnp.zeros((TOK, EXPERTS), F32)
        for i in range(4):
            w = wg[0, pl.ds(4 * i, 4)].reshape(896, EXPERTS)
            total = total + dot(x[:, pl.ds(896 * i, 896)], w)
        return sigmoid(total)

    score_f = scores(xf)
    score_b = scores(xb)
    sum_f = jnp.sum(mask_f * score_f, axis=1, keepdims=True)
    sum_b = jnp.sum(mask_b * score_b, axis=1, keepdims=True)
    gate_f = sel_f * to_slots(ROUTE_SCALE * score_f / sum_f)
    gate_b = sel_b * to_slots(ROUTE_SCALE * score_b / sum_b)
    msg[0], msg[1] = two_parts(gate_f)
    msg[2], msg[3] = two_parts(gate_b)
    mg = ids(1)
    push(msg, msg_in, at(y, pp=nxt), mg)

    for i in range(2):
        finish(i, out_b, pr_b, fs_b, fin_b, back_b, hs_b, hr_b)

    l_dot.wait()
    for k in range(1, 8):
        source = (mine + k) % 8
        got(got_dot.at[source], dt_r + source)
    all_dots = got_dot[...].reshape(FLIGHT, 2, CAP, 128)
    slot_dots = (all_dots[:, 0] + all_dots[:, 1]).reshape(SLOTS, 128)
    slot_row = lax.broadcasted_iota(jnp.int32, (SLOTS, EXPERTS), 0)
    slot_col = lax.broadcasted_iota(jnp.int32, (SLOTS, EXPERTS), 1)
    by_expert = jnp.where(
        slot_row // CAP == slot_col, jnp.broadcast_to(slot_dots[:, 0:1], (SLOTS, EXPERTS)), 0.0
    )
    gate_grad = exact(sel_b[:, :SLOTS], by_expert)
    weighted = jnp.sum(gate_grad * score_b, axis=1, keepdims=True) / sum_b
    pick_grad = ROUTE_SCALE / sum_b * (gate_grad - weighted)
    logit_grad = (mask_b * pick_grad * score_b * (1.0 - score_b)).astype(BF16)
    lg[...] = logit_grad
    lid = ids(1)
    push(lg, lg_in, at(y, pp=nxt), lid)

    def halves(fin, i):
        t = fin[i].astype(F32)
        return t[:, :CAP].reshape(SLOTS, PART).astype(BF16), t[:, CAP:].reshape(SLOTS, PART).astype(BF16)

    def arrived(fin, i, r_id):
        for k in range(4):
            source = (e + k) % 4
            got(fin.at[i, source], r_id + i * 4 + source)

    def router(i):
        return across(lg_in[...], wg[1, pl.ds(4 * i, 4)].reshape(PART, EXPERTS))

    got(msg_in, mg)
    f_high, f_low = msg_in[0][:, :SLOTS], msg_in[1][:, :SLOTS]
    b_high, b_low = msg_in[2][:, :SLOTS], msg_in[3][:, :SLOTS]
    for i in range(2):
        arrived(fin_f, i, hr_f)
        a, b = halves(fin_f, i)
        of_ref[:, pl.ds(i * PART, PART)] = (dot(f_high, a) + dot(f_low, a)).astype(BF16)
        of_ref[:, pl.ds(HALF + i * PART, PART)] = (dot(f_high, b) + dot(f_low, b)).astype(BF16)
    got(lg_in, lid)
    for i in range(2):
        arrived(fin_b, i, hr_b)
        a, b = halves(fin_b, i)
        ob_ref[:, pl.ds(i * PART, PART)] = (dot(b_high, a) + dot(b_low, a) + router(i)).astype(BF16)
        ob_ref[:, pl.ds(HALF + i * PART, PART)] = (dot(b_high, b) + dot(b_low, b) + router(2 + i)).astype(BF16)

    for cp in sends:
        cp.wait_send()


N_SEM = 192


def on_device(xf, xb, g, rf, rb, w, up, dn):
    vm = pltpu.VMEM
    scratch = [
        vm((TOK, D), BF16), vm((TOK, D), BF16), vm((TOK, D), BF16),
        vm((D, 4 * HID), BF16), vm((4 * HID, D), BF16), vm((2, 16, 2, WROWS, EXPERTS), BF16),
        vm((FLIGHT, 16, D), BF16), vm((FLIGHT, 16, HALF), BF16),
        vm((8, 16, D), BF16), vm((8, 16, HALF), BF16),
        vm((64, 4 * HID), F32), vm((64, 4 * HID), F32), vm((64, 4 * HID), F32),
        vm((8, CAP, 128), F32), vm((8, CAP, 128), F32),
        vm((2, 8, 16, PART), BF16), vm((2, 8, 16, PART), BF16),
        vm((2, 4, 16, PART), BF16), vm((2, 4, 16, PART), BF16),
        vm((2, 4, 16, PART), BF16), vm((2, 4, 16, PART), BF16),
        vm((2, 4, 16, PART), BF16), vm((2, 4, 16, PART), BF16),
        vm((4, TOK, 128), BF16), vm((4, TOK, 128), BF16),
        vm((TOK, EXPERTS), BF16), vm((TOK, EXPERTS), BF16),
        pltpu.SemaphoreType.DMA((16,)),
        pltpu.SemaphoreType.DMA((N_SEM,)),
        pltpu.SemaphoreType.DMA((N_SEM,)),
    ]
    hbm = pl.BlockSpec(memory_space=pl.ANY)
    vmem = pl.BlockSpec(memory_space=pltpu.VMEM)
    of, ob = pl.pallas_call(
        kernel,
        out_shape=[pltpu.VMEM((TOK, D), BF16)] * 2,
        in_specs=[hbm, hbm, hbm, vmem, vmem, hbm, hbm, hbm],
        out_specs=[vmem, vmem],
        scratch_shapes=scratch,
        compiler_params=pltpu.CompilerParams(
            collective_id=0, has_side_effects=True, vmem_limit_bytes=60 * 2**20
        ),
        cost_estimate=pl.CostEstimate(flops=2 * 10**9, bytes_accessed=6 * 10**6, transcendentals=10**5),
        name="expert_layer",
    )(xf[0], xb[0], g[0], rf[0].T, rb[0].T, w[0], up[0], dn[0])
    return of[None], ob[None]


def solution(mesh):
    rows = P("pipe", "expert", None)
    return jax.shard_map(
        on_device,
        mesh=mesh,
        in_specs=(rows, rows, rows, rows, rows, rows, P("pipe", None, "expert"), rows),
        out_specs=(rows, rows),
        check_vma=False,
    )
```

```python
import functools

import jax
import jax.numpy as jnp
from jax import lax
from jax.experimental import pallas as pl
from jax.experimental.pallas import tpu as pltpu
from jax.sharding import PartitionSpec as P

MESH = pl.DeviceIdType.MESH
D = 3584
HALF = D // 2
PART = HALF // 2
EXPERTS = 256
CAP = 8
FLIGHT = 4
SLOTS = FLIGHT * CAP
TOK = 64
HID = 128
WROWS = 112
NY = 8
DN = 4
SECTIONS = 16
ROUTE_SCALE = 2.5
HIGHEST = lax.Precision.HIGHEST
F32 = jnp.float32
BF16 = jnp.bfloat16
OFFSETS = (-1, 2, -3)


def across(a, b):
    return lax.dot_general(a, b, (((1,), (1,)), ((), ())), preferred_element_type=F32)


def dot(a, b):
    return jnp.dot(a, b, preferred_element_type=F32)


def exact(a, b):
    return jnp.dot(a, b, preferred_element_type=F32, precision=HIGHEST)


def sigmoid(v):
    return 1.0 / (1.0 + jnp.exp(-v))


def chosen_mask(routes_ref):
    wide = jnp.concatenate([routes_ref[...].astype(F32)] * 2, axis=1)
    routes = wide.T[:TOK]
    ids = lax.broadcasted_iota(jnp.int32, (TOK, EXPERTS), 1).astype(F32)
    mask = jnp.zeros((TOK, EXPERTS), F32)
    for k in range(routes_ref.shape[0]):
        mask = mask + jnp.where(routes[:, k : k + 1] == ids, 1.0, 0.0)
    return mask


def two_parts(v):
    high = v.astype(BF16)
    return high, (v - high.astype(F32)).astype(BF16)


def to_slots(columns):
    lane = lax.broadcasted_iota(jnp.int32, (TOK, 128), 1)
    out = jnp.zeros((TOK, 128), F32)
    for e in range(FLIGHT):
        inside = (lane >= e * CAP) & (lane < (e + 1) * CAP)
        out = out + jnp.where(inside, jnp.broadcast_to(columns[:, e : e + 1], (TOK, 128)), 0.0)
    return out


def slot_select(mask):
    member = to_slots(mask)
    row = lax.broadcasted_iota(jnp.int32, (TOK, TOK), 0)
    col = lax.broadcasted_iota(jnp.int32, (TOK, TOK), 1)
    below = jnp.where(col < row, 1.0, 0.0).astype(BF16)
    placing = dot(below, member.astype(BF16))
    lane = lax.broadcasted_iota(jnp.int32, (TOK, 128), 1)
    slot = (lane % CAP).astype(F32)
    return jnp.where(placing == slot, member, 0.0)


def kernel(
    xf_hbm, xb_hbm, g_hbm, rf_ref, rb_ref, w_hbm, up_hbm, dn_hbm,
    of_ref, ob_ref,
    xf, xb, g, up, dn, wg, pb, pf, rows_b, rows_f,
    pre_b, grad_b, pre_f, send_dot, got_dot, out_b, out_f,
    pr_b, pr_f, fs_b, fs_f, fin_b, fin_f,
    msg, msg_in, lg, lg_in,
    lsem, ssem, rsem,
):
    p = lax.axis_index("pipe")
    me = lax.axis_index("expert")
    y = me // 4
    xh = (me // 2) % 2
    c = me % 2
    e = y // 2
    sig = 1 - 2 * (y % 2)
    nxt = (p + 1) % SECTIONS
    prv = (p + SECTIONS - 1) % SECTIONS

    def at(yy, xx=None, cc=None, pp=None):
        xx = xh if xx is None else xx
        cc = c if cc is None else cc
        return (p if pp is None else pp, (yy * 2 + xx) * 2 + cc)

    def shift(off):
        return (y + NY + sig * off) % NY

    def slot_y(s):
        return shift(-s) if s < 4 else shift(s - 3)

    sib = at(y, cc=1 - c)
    xpart = at(y, xx=1 - xh)
    pair = at(shift(1))

    bar = pltpu.get_barrier_semaphore()

    def greet(dev):
        pl.semaphore_signal(bar, inc=1, device_id=dev, device_id_type=MESH)

    for s in range(1, 8):
        greet(at(slot_y(s)))
    greet(xpart)
    greet(sib)
    greet(at(y, pp=prv))
    greet(at(y, xx=1 - xh, pp=prv))
    for off in OFFSETS:
        greet(at(shift(off), pp=prv))

    nsem = [0]
    nlocal = [0]
    sends = []

    def ids(n):
        first = nsem[0]
        nsem[0] += n
        return first

    def local(src, dst):
        cp = pltpu.make_async_copy(src, dst, lsem.at[nlocal[0]])
        nlocal[0] += 1
        cp.start()
        return cp

    def push(src, dst, dev, s_id, r_id=None):
        cp = pltpu.make_async_remote_copy(
            src_ref=src, dst_ref=dst, send_sem=ssem.at[s_id],
            recv_sem=rsem.at[s_id if r_id is None else r_id],
            device_id=dev, device_id_type=MESH,
        )
        cp.start()
        sends.append(cp)

    def got(dst, r_id):
        pltpu.make_async_remote_copy(
            src_ref=dst, dst_ref=dst, send_sem=ssem.at[0], recv_sem=rsem.at[r_id],
            device_id=sib, device_id_type=MESH,
        ).wait_recv()

    l_xb = local(xb_hbm, xb)
    l_g = local(g_hbm, g)
    l_xf = local(xf_hbm, xf)
    l_up = local(up_hbm, up.at[:, pl.ds(0, HID)])
    l_dn = local(dn_hbm, dn.at[pl.ds(0, HID)])
    my_w = y * 2 + xh
    l_w = local(w_hbm, wg.at[0, my_w, c])

    mask_b = chosen_mask(rb_ref)
    mask_f = chosen_mask(rf_ref)
    sel_b = slot_select(mask_b)
    sel_f = slot_select(mask_f)
    pick_b = sel_b.T[:SLOTS].astype(BF16)
    pick_f = sel_f.T[:SLOTS].astype(BF16)

    l_xb.wait()
    l_g.wait()
    for i in range(7):
        cols = pl.ds(i * 512, 512)
        a = dot(pick_b, xb[:, cols]).reshape(FLIGHT, CAP, 512)
        b = dot(pick_b, g[:, cols]).reshape(FLIGHT, CAP, 512)
        pb[:, :, cols] = jnp.concatenate([a, b], axis=1).astype(BF16)

    pl.semaphore_wait(bar, 14)

    def up_part(k, rows):
        return up.at[rows, pl.ds(k * HID, HID)]

    def dn_part(k, cols):
        return dn.at[pl.ds(k * HID, HID), cols]

    up_rows = [pl.ds(i * HALF, HALF) for i in range(2)]
    dn_cols = [pl.ds(i * PART, PART) for i in (0, 2, 1, 3)]
    ux, us, uy, dx, ds_, dy = ids(2), ids(2), ids(2), ids(DN), ids(DN), ids(DN)

    def enter(src, rows, iy):
        push(src.at[e], rows.at[4], pair, iy + 4)
        for off in OFFSETS:
            t = shift(off)
            push(src.at[t // 2], rows.at[abs(off)], at(t), iy + abs(off))
        return local(src.at[e], rows.at[0])

    def hands(rows, iy, slots):
        for s in slots:
            got(rows.at[s], iy + s)
            push(rows.at[s], rows.at[4 + s], pair, iy + 4 + s)

    iy_b, iy_f = ids(8), ids(8)
    l_b0 = enter(pb, rows_b, iy_b)
    for i in range(2):
        push(up_hbm.at[up_rows[i]], up_part(1, up_rows[i]), sib, us + i)
    for i in range(DN):
        push(dn_hbm.at[:, dn_cols[i]], dn_part(1, dn_cols[i]), sib, ds_ + i)
    wx = ids(3)
    push(w_hbm, wg.at[0, my_w, c], xpart, wx)
    push(w_hbm, wg.at[1, my_w, c], at(y, pp=nxt), wx + 1)
    push(w_hbm, wg.at[1, my_w, c], at(y, xx=1 - xh, pp=nxt), wx + 2)

    l_xf.wait()
    for i in range(7):
        lo = pl.ds(i * 256, 256)
        hi = pl.ds(HALF + i * 256, 256)
        a = dot(pick_f, xf[:, lo]).reshape(FLIGHT, CAP, 256)
        b = dot(pick_f, xf[:, hi]).reshape(FLIGHT, CAP, 256)
        pf[:, :, lo] = jnp.concatenate([a, b], axis=1).astype(BF16)

    l_f0 = enter(pf, rows_f, iy_f)

    up_dev, down_dev = at((y + 1) % NY), at((y + NY - 1) % NY)
    wr = ids(16)

    def ring(step):
        yu = (y + NY - step) % NY
        yd = (y + step) % NY
        for xx in range(2):
            if step < 3 or xx == 0:
                push(wg.at[:, yu * 2 + xx, c], wg.at[:, yu * 2 + xx, c], up_dev, wr + step * 2 + xx)
            if step < 3 or xx == 1:
                push(wg.at[:, yd * 2 + xx, c], wg.at[:, yd * 2 + xx, c], down_dev, wr + 8 + step * 2 + xx)

    wsib = ids(18)

    def to_sibling(idx, n):
        push(wg.at[:, idx, c], wg.at[:, idx, c], sib, wsib + n)

    def from_sibling(idx, n):
        got(wg.at[:, idx, 1 - c], wsib + n)

    def ring_blocks(step):
        yu = (y + NY - step - 1) % NY
        yd = (y + step + 1) % NY
        for xx in range(2):
            if step < 3 or xx == 0:
                yield yu * 2 + xx, step * 2 + xx
            if step < 3 or xx == 1:
                yield yd * 2 + xx, 8 + step * 2 + xx

    def ring_got(step):
        for idx, n in ring_blocks(step):
            got(wg.at[:, idx, c], wr + n)
            to_sibling(idx, n)

    own, other = pl.ds(0, 2 * HID), pl.ds(2 * HID, 2 * HID)

    def forward_pre(lanes):
        r = rows_f[...].reshape(128, HALF)
        low = dot(r, up[pl.ds(0, HALF), lanes]).reshape(8, 16, 256)[:, :CAP]
        high = dot(r, up[pl.ds(HALF, HALF), lanes]).reshape(8, 16, 256)[:, CAP:]
        pre_f[:, lanes] = (low + high).reshape(64, 256)

    def backward_pre(lanes):
        r = rows_b[...].reshape(128, D)
        pre_b[:, lanes] = dot(r, up[:, lanes]).reshape(8, 16, 256)[:, :CAP].reshape(64, 256)

    def backward_grad(lanes):
        r = rows_b[...].reshape(128, D)
        grad_b[:, lanes] = across(r, dn[lanes, :]).reshape(8, 16, 256)[:, CAP:].reshape(64, 256)


    def up_on(i):
        got(up_part(2, up_rows[i]), ux + i)
        push(up_part(2, up_rows[i]), up_part(3, up_rows[i]), sib, uy + i)

    def dn_on(i):
        got(dn_part(2, dn_cols[i]), dx + i)
        push(dn_part(2, dn_cols[i]), dn_part(3, dn_cols[i]), sib, dy + i)

    def send_up(i):
        push(up_hbm.at[up_rows[i]], up_part(2, up_rows[i]), xpart, ux + i)

    def send_dn(i):
        push(dn_hbm.at[:, dn_cols[i]], dn_part(2, dn_cols[i]), xpart, dx + i)

    send_up(0)
    send_up(1)
    for i in range(DN):
        send_dn(i)
    hands(rows_b, iy_b, (1,))
    l_w.wait()
    their_w = y * 2 + (1 - xh)
    got(wg.at[0, their_w, c], wx)
    got(wg.at[1, my_w, c], wx + 1)
    got(wg.at[1, their_w, c], wx + 2)
    ring(0)
    to_sibling(my_w, 16)
    to_sibling(their_w, 17)
    hands(rows_b, iy_b, (2, 3))
    hands(rows_f, iy_f, (1, 2, 3))
    ring_got(0)
    ring(1)
    l_b0.wait()
    l_f0.wait()
    l_up.wait()
    l_dn.wait()
    for i in range(2):
        got(up_part(1, up_rows[i]), us + i)
    for i in range(DN):
        got(dn_part(1, dn_cols[i]), ds_ + i)
    for s in range(4, 8):
        got(rows_b.at[s], iy_b + s)
    backward_pre(own)
    backward_grad(own)
    ring_got(1)
    ring(2)
    up_on(0)
    for s in range(4, 8):
        got(rows_f.at[s], iy_f + s)
    forward_pre(own)
    ring_got(2)
    ring(3)
    up_on(1)
    for i in range(2):
        got(up_part(3, up_rows[i]), uy + i)
    backward_pre(other)
    forward_pre(other)
    back_b, back_f = ids(2), ids(2)
    pre = pre_f[...]
    act_f = (pre * sigmoid(pre)).astype(BF16)

    def forward_out(i):
        for j in (2 * i, 2 * i + 1):
            dn_on(j)
        for j in (2 * i, 2 * i + 1):
            got(dn_part(3, dn_cols[j]), dy + j)
        a = dot(act_f, dn[:, pl.ds(i * PART, PART)]).reshape(8, CAP, PART)
        b = dot(act_f, dn[:, pl.ds(HALF + i * PART, PART)]).reshape(8, CAP, PART)
        out_f[i] = jnp.concatenate([a, b], axis=1).astype(BF16)
        push(out_f.at[i, pl.ds(4, 4)], pr_f.at[i], pair, back_f + i)
        share = jnp.zeros((128, 2 * HID), F32)
        for j in (2 * i, 2 * i + 1):
            share = share + across(rows_b[:, :, dn_cols[j]].reshape(128, PART), dn[other, dn_cols[j]])
        share = share.reshape(8, 16, 2 * HID)[:, CAP:].reshape(64, 2 * HID)
        grad_b[:, other] = share if i == 0 else grad_b[:, other] + share

    forward_out(0)
    ring_got(3)
    forward_out(1)
    pre = pre_b[...]
    act_grad = grad_b[...]
    s = sigmoid(pre)
    act = (pre * s).astype(BF16).astype(F32)
    dots = jnp.sum(act * act_grad, axis=1, keepdims=True)
    send_dot[...] = jnp.broadcast_to(dots, (64, 128)).reshape(8, CAP, 128)
    pre_grad = (act_grad * (s * (1.0 + pre * (1.0 - s)))).astype(BF16)
    for i in range(2):
        a = across(pre_grad, up[pl.ds(i * PART, PART), :]).reshape(8, CAP, PART)
        b = across(pre_grad, up[pl.ds(HALF + i * PART, PART), :]).reshape(8, CAP, PART)
        out_b[i] = jnp.concatenate([a, b], axis=1).astype(BF16)
        push(out_b.at[i, pl.ds(4, 4)], pr_b.at[i], pair, back_b + i)
    mine = e * 2 + y % 2
    dt_s, dt_r = ids(8), ids(8)
    for k in range(1, 8):
        push(send_dot.at[k], got_dot.at[mine], at(slot_y(k)), dt_s + k, dt_r + mine)
    l_dot = local(send_dot.at[0], got_dot.at[mine])

    hs_b, hr_b, hs_f, hr_f = ids(8), ids(8), ids(8), ids(8)

    def finish(i, out, pr, fs, fin, arrived, s_id, r_id):
        got(pr.at[i], arrived + i)
        for k in (3, 2, 1, 0):
            fs[i, k] = (out[i, k].astype(F32) + pr[i, k].astype(F32)).astype(BF16)
            push(fs.at[i, k], fin.at[i, e], at(shift(-k), pp=nxt), s_id + i * 4 + k, r_id + i * 4 + e)

    for i in range(2):
        finish(i, out_f, pr_f, fs_f, fin_f, back_f, hs_f, hr_f)

    from_sibling(my_w, 16)
    from_sibling(their_w, 17)
    for step in range(4):
        for idx, n in ring_blocks(step):
            from_sibling(idx, n)

    def scores(x):
        total = jnp.zeros((TOK, EXPERTS), F32)
        for i in range(4):
            w = wg[0, pl.ds(4 * i, 4)].reshape(896, EXPERTS)
            total = total + dot(x[:, pl.ds(896 * i, 896)], w)
        return sigmoid(total)

    score_f = scores(xf)
    score_b = scores(xb)
    sum_f = jnp.sum(mask_f * score_f, axis=1, keepdims=True)
    sum_b = jnp.sum(mask_b * score_b, axis=1, keepdims=True)
    gate_f = sel_f * to_slots(ROUTE_SCALE * score_f / sum_f)
    gate_b = sel_b * to_slots(ROUTE_SCALE * score_b / sum_b)
    msg[0], msg[1] = two_parts(gate_f)
    msg[2], msg[3] = two_parts(gate_b)
    mg = ids(1)
    push(msg, msg_in, at(y, pp=nxt), mg)

    for i in range(2):
        finish(i, out_b, pr_b, fs_b, fin_b, back_b, hs_b, hr_b)

    l_dot.wait()
    for k in range(1, 8):
        source = (mine + k) % 8
        got(got_dot.at[source], dt_r + source)
    all_dots = got_dot[...].reshape(FLIGHT, 2, CAP, 128)
    slot_dots = (all_dots[:, 0] + all_dots[:, 1]).reshape(SLOTS, 128)
    slot_row = lax.broadcasted_iota(jnp.int32, (SLOTS, EXPERTS), 0)
    slot_col = lax.broadcasted_iota(jnp.int32, (SLOTS, EXPERTS), 1)
    by_expert = jnp.where(
        slot_row // CAP == slot_col, jnp.broadcast_to(slot_dots[:, 0:1], (SLOTS, EXPERTS)), 0.0
    )
    gate_grad = exact(sel_b[:, :SLOTS], by_expert)
    weighted = jnp.sum(gate_grad * score_b, axis=1, keepdims=True) / sum_b
    pick_grad = ROUTE_SCALE / sum_b * (gate_grad - weighted)
    logit_grad = (mask_b * pick_grad * score_b * (1.0 - score_b)).astype(BF16)
    lg[...] = logit_grad
    lid = ids(1)
    push(lg, lg_in, at(y, pp=nxt), lid)

    def halves(fin, i):
        t = fin[i].astype(F32)
        return t[:, :CAP].reshape(SLOTS, PART).astype(BF16), t[:, CAP:].reshape(SLOTS, PART).astype(BF16)

    def arrived(fin, i, r_id):
        for k in range(4):
            source = (e + k) % 4
            got(fin.at[i, source], r_id + i * 4 + source)

    def router(i):
        return across(lg_in[...], wg[1, pl.ds(4 * i, 4)].reshape(PART, EXPERTS))

    got(msg_in, mg)
    f_high, f_low = msg_in[0][:, :SLOTS], msg_in[1][:, :SLOTS]
    b_high, b_low = msg_in[2][:, :SLOTS], msg_in[3][:, :SLOTS]
    for i in range(2):
        arrived(fin_f, i, hr_f)
        a, b = halves(fin_f, i)
        of_ref[:, pl.ds(i * PART, PART)] = (dot(f_high, a) + dot(f_low, a)).astype(BF16)
        of_ref[:, pl.ds(HALF + i * PART, PART)] = (dot(f_high, b) + dot(f_low, b)).astype(BF16)
    got(lg_in, lid)
    for i in range(2):
        arrived(fin_b, i, hr_b)
        a, b = halves(fin_b, i)
        ob_ref[:, pl.ds(i * PART, PART)] = (dot(b_high, a) + dot(b_low, a) + router(i)).astype(BF16)
        ob_ref[:, pl.ds(HALF + i * PART, PART)] = (dot(b_high, b) + dot(b_low, b) + router(2 + i)).astype(BF16)

    for cp in sends:
        cp.wait_send()


N_SEM = 192


def on_device(xf, xb, g, rf, rb, w, up, dn):
    vm = pltpu.VMEM
    scratch = [
        vm((TOK, D), BF16), vm((TOK, D), BF16), vm((TOK, D), BF16),
        vm((D, 4 * HID), BF16), vm((4 * HID, D), BF16), vm((2, 16, 2, WROWS, EXPERTS), BF16),
        vm((FLIGHT, 16, D), BF16), vm((FLIGHT, 16, HALF), BF16),
        vm((8, 16, D), BF16), vm((8, 16, HALF), BF16),
        vm((64, 4 * HID), F32), vm((64, 4 * HID), F32), vm((64, 4 * HID), F32),
        vm((8, CAP, 128), F32), vm((8, CAP, 128), F32),
        vm((2, 8, 16, PART), BF16), vm((2, 8, 16, PART), BF16),
        vm((2, 4, 16, PART), BF16), vm((2, 4, 16, PART), BF16),
        vm((2, 4, 16, PART), BF16), vm((2, 4, 16, PART), BF16),
        vm((2, 4, 16, PART), BF16), vm((2, 4, 16, PART), BF16),
        vm((4, TOK, 128), BF16), vm((4, TOK, 128), BF16),
        vm((TOK, EXPERTS), BF16), vm((TOK, EXPERTS), BF16),
        pltpu.SemaphoreType.DMA((16,)),
        pltpu.SemaphoreType.DMA((N_SEM,)),
        pltpu.SemaphoreType.DMA((N_SEM,)),
    ]
    hbm = pl.BlockSpec(memory_space=pl.ANY)
    vmem = pl.BlockSpec(memory_space=pltpu.VMEM)
    of, ob = pl.pallas_call(
        kernel,
        out_shape=[pltpu.VMEM((TOK, D), BF16)] * 2,
        in_specs=[hbm, hbm, hbm, vmem, vmem, hbm, hbm, hbm],
        out_specs=[vmem, vmem],
        scratch_shapes=scratch,
        compiler_params=pltpu.CompilerParams(
            collective_id=0, has_side_effects=True, vmem_limit_bytes=60 * 2**20
        ),
        cost_estimate=pl.CostEstimate(flops=2 * 10**9, bytes_accessed=6 * 10**6, transcendentals=10**5),
        name="expert_layer",
    )(xf[0], xb[0], g[0], rf[0].T, rb[0].T, w[0], up[0], dn[0])
    return of[None], ob[None]


def solution(mesh):
    rows = P("pipe", "expert", None)
    return jax.shard_map(
        on_device,
        mesh=mesh,
        in_specs=(rows, rows, rows, rows, rows, rows, P("pipe", None, "expert"), rows),
        out_specs=(rows, rows),
        check_vma=False,
    )
```
